128 devices in a mesh: lat: 16 (over x, y), lev: 8 (over z, core).
Axes of the slice: x: 4, y: 4, z: 4, core: 2. Of those that a mesh axis runs over, the one named last changes fastest.
Arguments:
- fields: bfloat16 [64, 72, 16384], P('lat', None, 'lev'), may hold values from -6 to 6
- lat_order: int32 [64], replicated, may hold values from 0 to 63, each once
- counts: int32 [64], replicated, may hold values from 20 to 16016, as said below
- wave_order: int32 [2048], replicated, may hold values from 0 to 2047, as said below
- weights: float32 [64], replicated, may hold values from 0.3 to 3
- diffusion: float32 [3], replicated, may hold values from 0.5 to 8
- legendre: float32 [2048, 64, 2048], P(('lat', 'lev')), as said below
Outputs:
- fields_out: bfloat16 [64, 72, 16384], P('lat', None, 'lev')
The draws below stay inside these ranges and needn't reach their ends.
Inputs may be any that keep to these rules, and one draw needn't show every extreme that they name: counts are 4 i + 20 for distinct hemisphere rows i below 4000, rising with the latitude index, the first one the row i = 0, the last one the row i = 3999. `wave_order`: a permutation; the device at position s of lat+lev (lat slowest) owns the wavenumbers at positions s * 2048 / 128 up to the next set's first. `legendre`: entry [r, j, q] is 0 where q >= 2048 - wave_order_r.
All inputs are finite; a program needn't handle non-finite values.
Results may differ from the reference program's by a relative error of at most 0.006.
Values may be sent and summed in bfloat16 or wider, within the bound.
A program may use at most 128 MiB of HBM per device.

```python
import math
import jax
import jax.numpy as jnp
from jax import lax

M = 2048
HEMI = 4000
LEV = 24
NLAT = 64
FL = 72
CAP = 16384
N_LAT = 16
N_LEV = 8


def wave_permutation(key):
    return jax.random.permutation(jax.random.fold_in(key, 101), M).astype(jnp.int32)


def draw_wave_order(key, part):
    return wave_permutation(key)


def draw_legendre(key, part):
    wave_ids = wave_permutation(key)
    key = jax.random.fold_in(key, 202)
    spread = (2.0 * HEMI) ** 0.25 / (M * NLAT ** 0.5) ** 0.5
    values = jax.random.normal(key, (M, NLAT, M), jnp.float32) * spread
    degree = jnp.arange(M, dtype=jnp.int32)
    valid = degree[None, :] < (M - wave_ids)[:, None]
    return jnp.where(valid[:, None, :], values, 0.0).astype(jnp.float32)


def draw_counts(key, part):
    key = jax.random.fold_in(key, 303)
    picked = (jax.random.permutation(key, HEMI - 2)[:NLAT - 2] + 1).astype(jnp.int32)
    rows_used = jnp.concatenate([jnp.zeros((1,), jnp.int32), jnp.sort(picked), jnp.full((1,), HEMI - 1, jnp.int32)])
    return (4 * rows_used + 20).astype(jnp.int32)


def block_scale(rng, dims, split, low, largest):
    factor_of = 1.0
    for dim, shards_of in split:
        heights = jax.random.uniform(jax.random.fold_in(jax.random.fold_in(rng, 6), dim), (shards_of,), jnp.float32, low / len(split), largest / len(split))
        factor_of = factor_of * jnp.repeat(jnp.exp(heights), dims[dim] // shards_of).reshape((-1,) + (1,) * (len(dims) - 1 - dim))
    return factor_of


def centred(own_key, extent, scale, most, cuts=(), held_as=jnp.bfloat16):
    values = scale * jax.random.normal(own_key, extent, jnp.float32)
    if cuts:
        values = values * block_scale(own_key, extent, cuts, -0.22, 0.18)
    return jnp.clip(values, -most, most).astype(held_as)


def setup_inputs(seed: int = 0) -> dict:
    splits = jax.random.split(jax.random.key(seed), 8)
    return {
        "fields": centred(splits[0], (NLAT, FL, CAP), 1.0, 6.0, ((0, 16), (2, 8))),
        "lat_order": jax.random.permutation(splits[1], NLAT).astype(jnp.int32),
        "counts": draw_counts(jax.random.fold_in(splits[7], 71), 0),
        "wave_order": draw_wave_order(jax.random.fold_in(splits[7], 71), 0),
        "weights": jnp.clip(jnp.exp(jax.random.uniform(splits[4], (NLAT,), jnp.float32, math.log(0.3), math.log(3.0))), 0.3, 3.0),
        "diffusion": jnp.clip(jnp.exp(jax.random.uniform(splits[5], (3,), jnp.float32, math.log(0.5), math.log(8.0))), 0.5, 8.0),
        "legendre": draw_legendre(jax.random.fold_in(splits[7], 71), 0),
    }


full_turn = 2.0 * math.pi


def phase_table(wave_ids, row_count, positions, stride):
    turns = (wave_ids[None, :] * (stride * positions[:, None])) % row_count
    return full_turn * turns.astype(jnp.float32) / row_count.astype(jnp.float32)


def basis_table(wave_ids, row_count):
    angle = phase_table(wave_ids, row_count, jnp.arange(128, dtype=jnp.int32), 1)
    return jnp.concatenate([jnp.cos(angle), -jnp.sin(angle)], axis=1).astype(jnp.bfloat16)


def forward_row(points, row_count, wave_ids):
    row_width = points.shape[-1]
    blocks = row_width // 128
    wave_count = wave_ids.shape[0]
    inside = jnp.arange(row_width, dtype=jnp.int32) < row_count
    masked = jnp.where(inside[None, :], points, jnp.zeros((), points.dtype))
    partial_value = jnp.dot(masked.reshape(-1, 128), basis_table(wave_ids, row_count), preferred_element_type=jnp.float32)
    partial_value = partial_value.reshape(points.shape[0], blocks, 2 * wave_count)
    outer = phase_table(wave_ids, row_count, jnp.arange(blocks, dtype=jnp.int32), 128)
    cos_part, sin_part = jnp.cos(outer), jnp.sin(outer)
    real_in, imag_in = partial_value[..., :wave_count], partial_value[..., wave_count:]
    real_part = jnp.sum(real_in * cos_part + imag_in * sin_part, axis=1)
    imag_part = jnp.sum(imag_in * cos_part - real_in * sin_part, axis=1)
    cutoff = jnp.minimum(wave_count - 1, (row_count - 1) // 2)
    kept_share = jnp.where(wave_ids <= cutoff, 1.0, 0.0).astype(jnp.float32) / row_count.astype(jnp.float32)
    return jnp.stack([real_part, imag_part], axis=1) * kept_share


def inverse_row(coeffs, row_count, wave_ids, row_width):
    blocks = row_width // 128
    wave_count = wave_ids.shape[0]
    double = jnp.where(wave_ids == 0, 1.0, 2.0).astype(jnp.float32)
    real_in = coeffs[:, 0] * double
    imag_in = coeffs[:, 1] * double
    outer = phase_table(wave_ids, row_count, jnp.arange(blocks, dtype=jnp.int32), 128)
    cos_part, sin_part = jnp.cos(outer), jnp.sin(outer)
    real_twist = real_in[:, None, :] * cos_part - imag_in[:, None, :] * sin_part
    imag_twist = real_in[:, None, :] * sin_part + imag_in[:, None, :] * cos_part
    twisted = jnp.concatenate([real_twist, imag_twist], axis=-1).astype(jnp.bfloat16)
    values = lax.dot_general(twisted.reshape(-1, 2 * wave_count), basis_table(wave_ids, row_count), (((1,), (1,)), ((), ())), preferred_element_type=jnp.float32)
    values = values.reshape(coeffs.shape[0], row_width)
    inside = jnp.arange(row_width, dtype=jnp.int32) < row_count
    return jnp.where(inside[None, :], values, 0.0).astype(jnp.bfloat16)


def spectral_block(inputs, basis, wave_ids, counts, weights, diffusion, levels):
    batch_size, field_cols = inputs.shape[0], inputs.shape[1]
    total = basis.shape[2]
    weighted = (inputs * weights).reshape(batch_size, 2 * field_cols, -1)
    spectral = jnp.einsum("icj,ijq->icq", weighted, basis, precision=lax.Precision.HIGHEST)
    degree = wave_ids[:, None] + jnp.arange(total, dtype=jnp.int32)[None, :]
    scaled_degree = degree.astype(jnp.float32) * (degree + 1).astype(jnp.float32) / float(total * (total - 1))
    column_field = (jnp.arange(2 * field_cols, dtype=jnp.int32) // 2) // levels
    coefficient = jnp.take(diffusion, column_field)
    damping = 1.0 / (1.0 + coefficient[None, :, None] * (scaled_degree * scaled_degree)[:, None, :])
    returned = jnp.einsum("icq,ijq->icj", spectral * damping, basis, precision=lax.Precision.HIGHEST)
    cutoff = jnp.minimum(total - 1, (counts - 1) // 2)
    kept_share = jnp.where(wave_ids[:, None] <= cutoff[None, :], 1.0, 0.0).astype(jnp.float32)
    return (returned * kept_share[:, None, :]).reshape(batch_size, field_cols, 2, -1)


def reference(fields, lat_order, counts, wave_order, weights, diffusion, legendre):
    slot_counts = jnp.take(counts, lat_order)
    fourier = lax.map(lambda record: forward_row(record[0], record[1], wave_order), (fields, slot_counts))
    inverse = jnp.argsort(lat_order).astype(jnp.int32)
    by_latitude = jnp.take(fourier, inverse, axis=0)
    inputs = jnp.transpose(by_latitude, (3, 1, 2, 0))
    set_count = N_LAT * N_LEV
    each_set = M // set_count
    result = lax.map(
        lambda record: spectral_block(record[0], record[1], record[2], counts, weights, diffusion, LEV),
        (inputs.reshape(set_count, each_set, FL, 2, NLAT), legendre.reshape(set_count, each_set, NLAT, M), wave_order.reshape(set_count, each_set)))
    returned = result.reshape(M, FL, 2, NLAT)
    by_slot = jnp.transpose(jnp.take(returned, lat_order, axis=3), (3, 1, 2, 0))
    return lax.map(lambda record: inverse_row(record[0], record[1], wave_order, CAP), (by_slot, slot_counts))
```

```python
import math

import jax
import jax.numpy as jnp
from jax import lax
from jax.experimental import pallas as pl
from jax.experimental.pallas import tpu as pltpu
from jax.sharding import PartitionSpec as P

F32, BF16 = jnp.float32, jnp.bfloat16
MESH = pl.DeviceIdType.MESH

M = 2048
N_LAT, N_LEV = 16, 8
DEV = N_LAT * N_LEV
NLAT = 64
LEV = 24
FL = 72
HALF = FL // 2
ROWS = NLAT // N_LAT
PTS = 2048
K0 = 256
KK = PTS // K0
PAIRS = KK // 2
BLK = KK * HALF
EACH = M // DEV
WT = 256
LANES = 128


def nt_dot(a, b):
    return lax.dot_general(a, b, (((1,), (1,)), ((), ())), preferred_element_type=F32)


def sincos(wave, factor, count):
    product = wave * factor
    countf = count.astype(F32)
    turns = jnp.floor(product.astype(F32) * (1.0 / countf) + 0.5).astype(jnp.int32)
    rest = product - turns * count
    rest = jnp.where(2 * rest > count, rest - count, rest)
    rest = jnp.where(2 * rest < -count, rest + count, rest)
    z = rest.astype(F32) * (math.pi / countf)
    y = z * z
    s = jnp.full_like(y, 1.0 / math.factorial(13))
    for k in (11, 9, 7, 5, 3, 1):
        s = s * y + (-1.0) ** (k // 2) / math.factorial(k)
    s = s * z
    c = jnp.full_like(y, 1.0 / math.factorial(14) * -1.0)
    for k in (12, 10, 8, 6, 4, 2, 0):
        c = c * y + (-1.0) ** (k // 2) / math.factorial(k)
    return 1.0 - 2.0 * s * s, 2.0 * s * c


def kernel(
    lat_s, cnt_s, wave_s, wgt_s, dif_s, wave_v, fields, leg_hbm, out,
    leg, tmp, stage, xs, xr, basis, twc, tws, ebc, ebs, eac, eas, one,
    accr, acci, ft, fs, fr, x32, y32, rs, rr, pm, cn, wt, bs, gst, ur, ui, ys, yr, o32,
    leg_sem, xs_sem, xr_sem, fs_sem, fr_sem, rs_sem, rr_sem, ys_sem, yr_sem,
):
    lat, lev = lax.axis_index("lat"), lax.axis_index("lev")
    me = lat * N_LEV + lev
    z, core = lev // 2, lax.rem(lev, 2)

    barrier = pltpu.get_barrier_semaphore()

    def greet(d, carry):
        target = lax.rem(me + d, DEV)
        pl.semaphore_signal(
            barrier, inc=1, device_id=(target // N_LEV, lax.rem(target, N_LEV)), device_id_type=MESH
        )
        return carry

    lax.fori_loop(1, DEV, greet, 0)
    leg_copy = pltpu.make_async_copy(leg_hbm, leg, leg_sem)
    leg_copy.start()

    lane = lax.broadcasted_iota(jnp.int32, (FL, K0), 1)

    def stage_row(t, carry):
        count = cnt_s[lat_s[ROWS * lat + t]]
        for kk in range(KK):
            x = fields[t, :, kk * K0 : (kk + 1) * K0].astype(F32)
            tmp[kk % 2] = jnp.where(lane + (lev * PTS + kk * K0) < count, x, 0.0)
            for h in range(2):
                stage[h, kk * HALF : (kk + 1) * HALF, :] = tmp[kk % 2, h * HALF : (h + 1) * HALF, :]
        for h in range(2):
            xs[2 * t + h] = stage[h].astype(BF16)
        return carry

    lax.fori_loop(0, ROWS, stage_row, 0)

    pl.semaphore_wait(barrier, DEV - 1)

    def x_copy(target, slot_sem_src, source):
        return pltpu.make_async_remote_copy(
            src_ref=xs.at[target],
            dst_ref=xr.at[source],
            send_sem=xs_sem.at[target],
            recv_sem=xr_sem.at[source],
            device_id=(lat, target),
            device_id_type=MESH,
        )

    def send_x(d, carry):
        target = lax.rem(lev + d, N_LEV)
        x_copy(target, None, lev).start()
        return carry

    lax.fori_loop(1, N_LEV, send_x, 0)

    count = cnt_s[lat_s[ROWS * lat + z]]
    waves16 = jnp.broadcast_to(wave_v[...], (16, M))
    row16 = lax.broadcasted_iota(jnp.int32, (16, M), 0)
    ebc[...], ebs[...] = sincos(waves16, row16, count)
    eac[...], eas[...] = sincos(waves16, row16 * 16, count)
    twc[0:16], tws[0:16] = sincos(waves16, row16 * (2 * K0), count)
    twc[16:32], tws[16:32] = sincos(waves16, row16 * (2 * K0) + 32 * K0, count)
    waves8 = jnp.broadcast_to(wave_v[...], (8, M))
    one[0], one[1] = sincos(waves8, jnp.full((8, M), K0, jnp.int32), count)

    def basis_rows(a, carry):
        ca, sa = eac[pl.ds(a, 1), :], eas[pl.ds(a, 1), :]
        cb, sb = ebc[...], ebs[...]
        rows = pl.ds(pl.multiple_of(a * 16, 16), 16)
        basis[rows, 0:M] = (ca * cb - sa * sb).astype(BF16)
        basis[rows, M : 2 * M] = (-(sa * cb + ca * sb)).astype(BF16)
        return carry

    lax.fori_loop(0, 16, basis_rows, 0)

    lane64 = lax.broadcasted_iota(jnp.int32, (1, NLAT), 1)

    def slot_row(t, carry):
        j = lat_s[t]
        row = pl.ds(t, 1)
        pm[row, :] = jnp.where(lane64 == j, 1.0, 0.0)
        cn[row, :] = jnp.full((1, NLAT), cnt_s[j], jnp.int32).astype(F32)
        wt[row, :] = jnp.full((1, NLAT), wgt_s[j], F32)
        return carry

    lax.fori_loop(0, NLAT, slot_row, 0)
    eye = lax.broadcasted_iota(jnp.int32, (NLAT, NLAT), 0) == lax.broadcasted_iota(
        jnp.int32, (NLAT, NLAT), 1
    )
    count_col = cn[...]
    count_row = jnp.sum(jnp.where(eye, count_col, 0.0), axis=0, keepdims=True)
    share_row = jnp.sum(jnp.where(eye, wt[...], 0.0), axis=0, keepdims=True) / count_row
    perm = pm[...].astype(BF16)
    degree = lax.broadcasted_iota(jnp.int32, (1, M), 1)
    leg_copy.wait()

    def operator(i, carry):
        m = wave_s[me * EACH + i]
        n = (degree + m).astype(F32)
        scaled = n * (n + 1.0) * (1.0 / float(M * (M - 1)))
        scaled = scaled * scaled
        own = jnp.dot(perm, leg[i].astype(BF16), preferred_element_type=F32)
        for f in range(3):
            bs[f * NLAT : (f + 1) * NLAT, :] = (own * (1.0 / (1.0 + dif_s[f] * scaled))).astype(BF16)
        g = nt_dot(bs[...], own.astype(BF16))
        twice_m = (2 * jnp.full((1, NLAT), m, jnp.int32)).astype(F32)
        from_row = jnp.where(twice_m < count_row, share_row, 0.0)
        to_col = jnp.where(twice_m < count_col, jnp.where(twice_m == 0.0, 1.0, 2.0), 0.0)
        scale = to_col * from_row
        for f in range(3):
            gst[i, f * NLAT : (f + 1) * NLAT, :] = (g[f * NLAT : (f + 1) * NLAT, :] * scale).astype(BF16)
        return carry

    lax.fori_loop(0, EACH, operator, 0)

    accr[...] = jnp.zeros_like(accr)
    acci[...] = jnp.zeros_like(acci)
    xr[lev] = xs[lev]

    def forward(p):
        points = xr[p]
        for w in range(M // WT):
            cols = slice(w * WT, (w + 1) * WT)
            pr = jnp.dot(points, basis[:, cols], preferred_element_type=F32)
            pi = jnp.dot(points, basis[:, M + w * WT : M + (w + 1) * WT], preferred_element_type=F32)
            ar, ai = accr[:, cols], acci[:, cols]
            for k in range(PAIRS):
                c = twc[pl.ds(p * PAIRS + k, 1), cols]
                s = tws[pl.ds(p * PAIRS + k, 1), cols]
                br, bi = pr[k * FL : (k + 1) * FL], pi[k * FL : (k + 1) * FL]
                ar = ar + (br * c + bi * s)
                ai = ai + (bi * c - br * s)
            accr[:, cols] = ar
            acci[:, cols] = ai

    forward(lev)

    def arrived(step, carry):
        chip_step = step // 2
        far = jnp.where(chip_step == 0, 0, jnp.where(chip_step == 1, 1, jnp.where(chip_step == 2, 3, 2)))
        p = 2 * lax.rem(z + far, 4) + lax.rem(core + lax.rem(step, 2), 2)
        x_copy(p, None, p).wait_recv()
        forward(p)
        return carry

    lax.fori_loop(1, N_LEV, arrived, 0)

    ft[FL:LANES, :] = jnp.zeros((LANES - FL, M), F32)
    c1, s1 = one[0, 0:1, :], one[1, 0:1, :]
    odd_r, odd_i = accr[HALF:FL, :], acci[HALF:FL, :]
    ft[0:HALF, :] = accr[0:HALF, :] + (odd_r * c1 + odd_i * s1)
    ft[HALF:FL, :] = acci[0:HALF, :] + (odd_i * c1 - odd_r * s1)
    for w in range(M // LANES):
        fs[w * LANES : (w + 1) * LANES, :] = ft[:, w * LANES : (w + 1) * LANES].T.astype(BF16)

    def tile(index):
        return pl.ds(pl.multiple_of(index * EACH, EACH), EACH)

    def send_tiles(source, target_ref, send_sem, recv_sem):
        def step(d, carry):
            target = lax.rem(me + d, DEV)
            pltpu.make_async_remote_copy(
                src_ref=source.at[tile(target), :],
                dst_ref=target_ref.at[tile(me), :],
                send_sem=send_sem,
                recv_sem=recv_sem,
                device_id=(target // N_LEV, lax.rem(target, N_LEV)),
                device_id_type=MESH,
            ).start()
            return carry

        lax.fori_loop(1, DEV, step, 0)
        target_ref[tile(me), :] = source[tile(me), :]

    def all_tiles(source, target_ref, send_sem, recv_sem):
        whole = pl.ds(0, (DEV - 1) * EACH)
        return pltpu.make_async_remote_copy(
            src_ref=source.at[whole, :],
            dst_ref=target_ref.at[whole, :],
            send_sem=send_sem,
            recv_sem=recv_sem,
            device_id=(lat, lax.rem(lev + 1, N_LEV)),
            device_id_type=MESH,
        )

    send_tiles(fs, fr, fs_sem, fr_sem)
    all_tiles(fs, fr, fs_sem, fr_sem).wait_recv()

    x32[...] = fr[...].astype(F32)
    column = lax.broadcasted_iota(jnp.int32, (NLAT, LANES), 1)
    column = jnp.where(column >= HALF, column - HALF, column)
    first_low, first_high = column < LEV, column < 2 * LEV - HALF
    for i in range(EACH):
        low = x32[pl.ds(i, NLAT, stride=2 * EACH), :]
        high = x32[pl.ds(EACH + i, NLAT, stride=2 * EACH), :]
        both = jnp.concatenate([low, high], axis=1).astype(BF16)
        y = jnp.dot(gst[i], both, preferred_element_type=F32)
        y32[pl.ds(i, NLAT, stride=2 * EACH), :] = jnp.where(
            first_low, y[0:NLAT, 0:LANES], y[NLAT : 2 * NLAT, 0:LANES]
        )
        y32[pl.ds(EACH + i, NLAT, stride=2 * EACH), :] = jnp.where(
            first_high, y[NLAT : 2 * NLAT, LANES:], y[2 * NLAT :, LANES:]
        )
    rs[...] = y32[...].astype(BF16)
    send_tiles(rs, rr, rs_sem, rr_sem)
    all_tiles(rs, rr, rs_sem, rr_sem).wait_recv()

    for w in range(M // LANES):
        cols = slice(w * LANES, (w + 1) * LANES)
        ft[:, cols] = rr[cols, :].astype(F32).T
    re, im = ft[0:HALF, :], ft[HALF:FL, :]
    ur[0:HALF, :] = re
    ui[0:HALF, :] = im
    ur[HALF:FL, :] = re * c1 - im * s1
    ui[HALF:FL, :] = re * s1 + im * c1

    row = lax.broadcasted_iota(jnp.int32, (BLK, K0), 0)
    point = lax.broadcasted_iota(jnp.int32, (BLK, K0), 1)
    for kk in range(1, KK):
        point = point + jnp.where(row >= kk * HALF, K0, 0)

    def inverse(p):
        total = jnp.zeros((BLK, K0), F32)
        for w in range(M // WT):
            cols = slice(w * WT, (w + 1) * WT)
            vr, vi = ur[:, cols], ui[:, cols]
            tr, ti = [], []
            for k in range(PAIRS):
                c = twc[pl.ds(p * PAIRS + k, 1), cols]
                s = tws[pl.ds(p * PAIRS + k, 1), cols]
                tr.append(vr * c - vi * s)
                ti.append(vr * s + vi * c)
            total = total + nt_dot(jnp.concatenate(tr, axis=0).astype(BF16), basis[:, cols])
            total = total + nt_dot(
                jnp.concatenate(ti, axis=0).astype(BF16), basis[:, M + w * WT : M + (w + 1) * WT]
            )
        ys[p] = jnp.where(point + p * PTS < count, total, 0.0).astype(BF16)

    def y_copy(target, source):
        return pltpu.make_async_remote_copy(
            src_ref=ys.at[target],
            dst_ref=yr.at[source],
            send_sem=ys_sem.at[target],
            recv_sem=yr_sem.at[source],
            device_id=(lat, target),
            device_id_type=MESH,
        )

    def made(step, carry):
        chip_step = step // 2
        far = jnp.where(chip_step == 0, 2, jnp.where(chip_step == 1, 1, jnp.where(chip_step == 2, 3, 0)))
        p = 2 * lax.rem(z + far, 4) + lax.rem(core + 1 + lax.rem(step, 2), 2)
        inverse(p)
        y_copy(p, lev).start()
        return carry

    lax.fori_loop(0, N_LEV - 1, made, 0)
    inverse(lev)
    yr[lev] = ys[lev]

    def waited(d, carry):
        y_copy(0, lax.rem(lev + d, N_LEV)).wait_recv()
        return carry

    lax.fori_loop(1, N_LEV, waited, 0)

    def finish_row(t, carry):
        for h in range(2):
            stage[h] = yr[2 * t + h].astype(F32)
        for kk in range(KK):
            for h in range(2):
                o32[h * HALF : (h + 1) * HALF, kk * K0 : (kk + 1) * K0] = stage[
                    h, kk * HALF : (kk + 1) * HALF, :
                ]
        out[t] = o32[...].astype(BF16)
        return carry

    lax.fori_loop(0, ROWS, finish_row, 0)

    def sent(d, carry):
        target = lax.rem(lev + d, N_LEV)
        x_copy(target, None, lev).wait_send()
        y_copy(target, lev).wait_send()
        return carry

    lax.fori_loop(1, N_LEV, sent, 0)
    all_tiles(fs, fr, fs_sem, fr_sem).wait_send()
    all_tiles(rs, rr, rs_sem, rr_sem).wait_send()


def body(fields, lat_order, counts, wave_order, weights, diffusion, legendre):
    smem, vmem = pl.BlockSpec(memory_space=pltpu.SMEM), pl.BlockSpec(memory_space=pltpu.VMEM)
    dma = pltpu.SemaphoreType.DMA
    block = pltpu.VMEM((N_LEV, BLK, K0), BF16)
    tiles16 = pltpu.VMEM((M, LANES), BF16)
    tiles32 = pltpu.VMEM((M, LANES), F32)
    acc = pltpu.VMEM((FL, M), F32)
    table = pltpu.VMEM((16, M), F32)
    square = pltpu.VMEM((NLAT, NLAT), F32)
    return pl.pallas_call(
        kernel,
        out_shape=jax.ShapeDtypeStruct(fields.shape, BF16),
        in_specs=[smem] * 5 + [vmem, vmem, pl.BlockSpec(memory_space=pl.ANY)],
        out_specs=vmem,
        scratch_shapes=[
            pltpu.VMEM((EACH, NLAT, M), F32),
            pltpu.VMEM((2, FL, K0), F32),
            pltpu.VMEM((2, BLK, K0), F32),
            block, block,
            pltpu.VMEM((K0, 2 * M), BF16),
            pltpu.VMEM((32, M), F32), pltpu.VMEM((32, M), F32),
            table, table, table, table,
            pltpu.VMEM((2, 8, M), F32),
            acc, acc,
            pltpu.VMEM((LANES, M), F32),
            tiles16, tiles16, tiles32, tiles32, tiles16, tiles16,
            square, square, square,
            pltpu.VMEM((3 * NLAT, M), BF16),
            pltpu.VMEM((EACH, 3 * NLAT, NLAT), BF16),
            acc, acc,
            block, block,
            acc,
            dma,
            dma((N_LEV,)), dma((N_LEV,)),
            dma, dma, dma, dma,
            dma((N_LEV,)), dma((N_LEV,)),
        ],
        compiler_params=pltpu.CompilerParams(
            collective_id=0, has_side_effects=True, vmem_limit_bytes=56 * 1024 * 1024
        ),
        cost_estimate=pl.CostEstimate(
            flops=20_000_000_000, bytes_accessed=12_000_000, transcendentals=0
        ),
    )(lat_order, counts, wave_order, weights, diffusion, wave_order.reshape(1, M), fields, legendre)


def solution(mesh):
    placed = (P("lat", None, "lev"), P(), P(), P(), P(), P(), P(("lat", "lev"), None, None))
    return jax.shard_map(
        body, mesh=mesh, in_specs=placed, out_specs=P("lat", None, "lev"), check_vma=False
    )
```

```python
import math

import jax
import jax.numpy as jnp
from jax import lax
from jax.experimental import pallas as pl
from jax.experimental.pallas import tpu as pltpu
from jax.sharding import PartitionSpec as P

F32, BF16 = jnp.float32, jnp.bfloat16
MESH = pl.DeviceIdType.MESH

M = 2048
N_LAT, N_LEV = 16, 8
DEV = N_LAT * N_LEV
NLAT = 64
LEV = 24
FL = 72
HALF = FL // 2
ROWS = NLAT // N_LAT
PTS = 2048
K0 = 256
KK = PTS // K0
PAIRS = KK // 2
EACH = M // DEV
WT = 256
LANES = 128
SIZES = (20, 16)
STARTS = (0, 20)
CHUNKS = range(len(SIZES))
SLOT = 64


def padded(rows):
    return -(-rows // 16) * 16


def nt_dot(a, b):
    return lax.dot_general(a, b, (((1,), (1,)), ((), ())), preferred_element_type=F32)


def sincos(wave, factor, count):
    product = wave * factor
    countf = count.astype(F32)
    turns = jnp.floor(product.astype(F32) * (1.0 / countf) + 0.5).astype(jnp.int32)
    rest = product - turns * count
    rest = jnp.where(2 * rest > count, rest - count, rest)
    rest = jnp.where(2 * rest < -count, rest + count, rest)
    z = rest.astype(F32) * (math.pi / countf)
    y = z * z
    s = jnp.full_like(y, 1.0 / math.factorial(13))
    for k in (11, 9, 7, 5, 3, 1):
        s = s * y + (-1.0) ** (k // 2) / math.factorial(k)
    s = s * z
    c = jnp.full_like(y, 1.0 / math.factorial(14) * -1.0)
    for k in (12, 10, 8, 6, 4, 2, 0):
        c = c * y + (-1.0) ** (k // 2) / math.factorial(k)
    return 1.0 - 2.0 * s * s, 2.0 * s * c


def kernel(
    lat_s, cnt_s, wave_s, wgt_s, dif_s, wave_v, fields, leg_hbm, out,
    leg, tmp, stages, xs, xr, basis, twc, tws, ebc, ebs, eac, eas, one,
    accr, acci, ft, fs, f1, mid, m1, f2, x32, y32, g1, g2, gs, g3,
    pm, cn, wt, bs, gst, ur, ui, ys, yr, o32,
    leg_sem, xs_sem, xr_sem, ys_sem, yr_sem, tile_sem,
):
    lat, lev = lax.axis_index("lat"), lax.axis_index("lev")
    z = lev // 2

    barrier = pltpu.get_barrier_semaphore()

    def greet_lev(d, carry):
        pl.semaphore_signal(
            barrier, inc=1, device_id=(lat, lax.rem(lev + d, N_LEV)), device_id_type=MESH
        )
        return carry

    def greet_lat(d, carry):
        pl.semaphore_signal(
            barrier, inc=1, device_id=(lax.rem(lat + d, N_LAT), lev), device_id_type=MESH
        )
        return carry

    lax.fori_loop(1, N_LEV, greet_lev, 0)
    lax.fori_loop(1, N_LAT, greet_lat, 0)
    leg_copy = pltpu.make_async_copy(leg_hbm, leg, leg_sem)
    leg_copy.start()

    lane = lax.broadcasted_iota(jnp.int32, (FL, K0), 1)

    def stage_row(t, carry):
        count = cnt_s[lat_s[ROWS * lat + t]]
        for kk in range(KK):
            x = fields[t, :, kk * K0 : (kk + 1) * K0].astype(F32)
            tmp[kk % 2] = jnp.where(lane + (lev * PTS + kk * K0) < count, x, 0.0)
            for n in CHUNKS:
                for h in range(2):
                    first = h * HALF + STARTS[n]
                    stages[n][h, kk * SIZES[n] : (kk + 1) * SIZES[n], :] = tmp[
                        kk % 2, first : first + SIZES[n], :
                    ]
        for n in CHUNKS:
            for h in range(2):
                xs[n][2 * t + h] = stages[n][h].astype(BF16)
        return carry

    lax.fori_loop(0, ROWS, stage_row, 0)

    pl.semaphore_wait(barrier, N_LEV - 1 + N_LAT - 1)

    def x_copy(n, target, source):
        return pltpu.make_async_remote_copy(
            src_ref=xs[n].at[target],
            dst_ref=xr[n].at[source],
            send_sem=xs_sem.at[n, target],
            recv_sem=xr_sem.at[n, source],
            device_id=(lat, target),
            device_id_type=MESH,
        )

    other = lev + 1 - 2 * lax.rem(lev, 2)

    def partner(step):
        chip_step = step // 2
        far = jnp.where(chip_step == 0, 1, jnp.where(chip_step == 1, 3, 2))
        return 2 * lax.rem(z + far, 4) + lax.rem(lev + lax.rem(step, 2), 2)

    for n in CHUNKS:
        x_copy(n, other, lev).start()

        def send_x(step, carry, n=n):
            x_copy(n, partner(step), lev).start()
            return carry

        lax.fori_loop(0, 6, send_x, 0)

    count = cnt_s[lat_s[ROWS * lat + z]]
    waves16 = jnp.broadcast_to(wave_v[...], (16, M))
    row16 = lax.broadcasted_iota(jnp.int32, (16, M), 0)
    ebc[...], ebs[...] = sincos(waves16, row16, count)
    eac[...], eas[...] = sincos(waves16, row16 * 16, count)
    twc[0:16], tws[0:16] = sincos(waves16, row16 * (2 * K0), count)
    twc[16:32], tws[16:32] = sincos(waves16, row16 * (2 * K0) + 32 * K0, count)
    waves8 = jnp.broadcast_to(wave_v[...], (8, M))
    one[0], one[1] = sincos(waves8, jnp.full((8, M), K0, jnp.int32), count)

    def basis_rows(a, carry):
        ca, sa = eac[pl.ds(a, 1), :], eas[pl.ds(a, 1), :]
        cb, sb = ebc[...], ebs[...]
        rows = pl.ds(pl.multiple_of(a * 16, 16), 16)
        basis[rows, 0:M] = (ca * cb - sa * sb).astype(BF16)
        basis[rows, M : 2 * M] = (-(sa * cb + ca * sb)).astype(BF16)
        return carry

    lax.fori_loop(0, 16, basis_rows, 0)

    lane64 = lax.broadcasted_iota(jnp.int32, (1, NLAT), 1)

    def slot_row(t, carry):
        j = lat_s[t]
        row = pl.ds(t, 1)
        pm[row, :] = jnp.where(lane64 == j, 1.0, 0.0)
        cn[row, :] = jnp.full((1, NLAT), cnt_s[j], jnp.int32).astype(F32)
        wt[row, :] = jnp.full((1, NLAT), wgt_s[j], F32)
        return carry

    lax.fori_loop(0, NLAT, slot_row, 0)
    eye = lax.broadcasted_iota(jnp.int32, (NLAT, NLAT), 0) == lax.broadcasted_iota(
        jnp.int32, (NLAT, NLAT), 1
    )
    count_col = cn[...]
    count_row = jnp.sum(jnp.where(eye, count_col, 0.0), axis=0, keepdims=True)
    share_row = jnp.sum(jnp.where(eye, wt[...], 0.0), axis=0, keepdims=True) / count_row
    perm = pm[...].astype(BF16)
    degree = lax.broadcasted_iota(jnp.int32, (1, M), 1)
    leg_copy.wait()

    def operator(i, carry):
        m = wave_s[(lat * N_LEV + lev) * EACH + i]
        deg = (degree + m).astype(F32)
        scaled = deg * (deg + 1.0) * (1.0 / float(M * (M - 1)))
        scaled = scaled * scaled
        own = jnp.dot(perm, leg[i].astype(BF16), preferred_element_type=F32)
        for f in range(3):
            bs[f * NLAT : (f + 1) * NLAT, :] = (own * (1.0 / (1.0 + dif_s[f] * scaled))).astype(BF16)
        g = nt_dot(bs[...], own.astype(BF16))
        twice_m = (2 * jnp.full((1, NLAT), m, jnp.int32)).astype(F32)
        from_row = jnp.where(twice_m < count_row, share_row, 0.0)
        to_col = jnp.where(twice_m < count_col, jnp.where(twice_m == 0.0, 1.0, 2.0), 0.0)
        scale = to_col * from_row
        for f in range(3):
            gst[i, f * NLAT : (f + 1) * NLAT, :] = (g[f * NLAT : (f + 1) * NLAT, :] * scale).astype(BF16)
        return carry

    lax.fori_loop(0, EACH, operator, 0)

    x32[...] = jnp.zeros_like(x32)
    ft[...] = jnp.zeros_like(ft)
    c1, s1 = one[0, 0:1, :], one[1, 0:1, :]

    def xy_copy(n, k, source, target_ref, d):
        target = lax.rem(lat + d, N_LAT)
        return pltpu.make_async_remote_copy(
            src_ref=source.at[target],
            dst_ref=target_ref.at[lat],
            send_sem=tile_sem.at[n, k, 0],
            recv_sem=tile_sem.at[n, k, 1],
            device_id=(target, lev),
            device_id_type=MESH,
        )

    def xy_send(n, k, source, target_ref):
        def step(d, carry):
            xy_copy(n, k, source, target_ref, d).start()
            return carry

        lax.fori_loop(1, N_LAT, step, 0)
        target_ref[lat] = source[lat]

    def xy_all(n, k, source, target_ref):
        return pltpu.make_async_remote_copy(
            src_ref=source.at[pl.ds(0, N_LAT - 1)],
            dst_ref=target_ref.at[pl.ds(0, N_LAT - 1)],
            send_sem=tile_sem.at[n, k, 0],
            recv_sem=tile_sem.at[n, k, 1],
            device_id=(lax.rem(lat + 1, N_LAT), lev),
            device_id_type=MESH,
        )

    def slab(index):
        return pl.ds(pl.multiple_of(index * EACH, EACH), EACH)

    def z_send(n, k, source, target_ref):
        def step(d, carry):
            target = lax.rem(lev + d, N_LEV)
            pltpu.make_async_remote_copy(
                src_ref=source.at[slab(target), :],
                dst_ref=target_ref.at[slab(lev), :],
                send_sem=tile_sem.at[n, k, 0],
                recv_sem=tile_sem.at[n, k, 1],
                device_id=(lat, target),
                device_id_type=MESH,
            ).start()
            return carry

        lax.fori_loop(1, N_LEV, step, 0)
        target_ref[slab(lev), :] = source[slab(lev), :]

    def z_all(n, k, source, target_ref):
        whole = pl.ds(0, (N_LEV - 1) * EACH)
        return pltpu.make_async_remote_copy(
            src_ref=source.at[whole, :],
            dst_ref=target_ref.at[whole, :],
            send_sem=tile_sem.at[n, k, 0],
            recv_sem=tile_sem.at[n, k, 1],
            device_id=(lat, lax.rem(lev + 1, N_LEV)),
            device_id_type=MESH,
        )

    def chip_at(step):
        far = jnp.where(step == 0, 0, jnp.where(step == 1, 3, jnp.where(step == 2, 1, 2)))
        return lax.rem(z + far, 4)

    def forward_start(n):
        accr[n][...] = jnp.zeros_like(accr[n])
        acci[n][...] = jnp.zeros_like(acci[n])
        xr[n][lev] = xs[n][lev]

    def forward(n, first, last):
        columns = 2 * SIZES[n]

        def step(index, carry):
            chip = chip_at(index)
            for q in range(2):
                p = 2 * chip + q

                @pl.when(p != lev)
                def _(p=p):
                    x_copy(n, p, p).wait_recv()

            points = xr[n][pl.ds(2 * chip, 2)].reshape(2 * KK * SIZES[n], K0)
            for w in range(M // WT):
                cols = slice(w * WT, (w + 1) * WT)
                pr = jnp.dot(points, basis[:, cols], preferred_element_type=F32)
                pi = jnp.dot(points, basis[:, M + w * WT : M + (w + 1) * WT], preferred_element_type=F32)
                ar, ai = accr[n][:, cols], acci[n][:, cols]
                for k in range(2 * PAIRS):
                    c = twc[pl.ds(chip * (2 * PAIRS) + k, 1), cols]
                    s = tws[pl.ds(chip * (2 * PAIRS) + k, 1), cols]
                    br, bi = pr[k * columns : (k + 1) * columns], pi[k * columns : (k + 1) * columns]
                    ar = ar + (br * c + bi * s)
                    ai = ai + (bi * c - br * s)
                accr[n][:, cols] = ar
                acci[n][:, cols] = ai
            return carry

        lax.fori_loop(first, last, step, 0)

    def forward_end(n):
        size, columns = SIZES[n], 2 * SIZES[n]
        odd_r, odd_i = accr[n][size:columns, :], acci[n][size:columns, :]
        ft[0:size, :] = accr[n][0:size, :] + (odd_r * c1 + odd_i * s1)
        ft[size:columns, :] = acci[n][0:size, :] + (odd_i * c1 - odd_r * s1)
        for w in range(N_LAT):
            fs[n][w] = ft[0 : padded(columns), w * LANES : (w + 1) * LANES].astype(BF16)
        xy_send(n, 0, fs[n], f1[n])

    def middle(n):
        columns = 2 * SIZES[n]
        xy_all(n, 0, fs[n], f1[n]).wait_recv()
        for r in range(N_LAT):
            mid[r * columns : (r + 1) * columns, :] = f1[n][r].astype(F32)[0:columns, :]
        for j in range(N_LAT * columns // LANES):
            cols = slice(j * LANES, (j + 1) * LANES)
            m1[n][:, cols] = mid[cols, :].T.astype(BF16)
        z_send(n, 1, m1[n], f2[n])

    def apply(n):
        size, columns = SIZES[n], 2 * SIZES[n]
        z_all(n, 1, m1[n], f2[n]).wait_recv()
        for source in range(N_LEV):
            v = f2[n][source * EACH : (source + 1) * EACH, :].astype(F32)
            lanes = slice((source % 2) * SLOT, (source % 2) * SLOT + columns)
            for r in range(N_LAT):
                t = r * ROWS + source // 2
                x32[t * EACH : (t + 1) * EACH, lanes] = v[:, r * columns : (r + 1) * columns]
        column = lax.broadcasted_iota(jnp.int32, (NLAT, LANES), 1)
        level = STARTS[n] + jnp.where(column >= SLOT, column - SLOT + HALF, column)
        inside = jnp.where(column >= SLOT, column - SLOT, column)
        level = jnp.where(inside >= size, level - size, level)
        for i in range(EACH):
            x = x32[pl.ds(i, NLAT, stride=EACH), :].astype(BF16)
            y = jnp.dot(gst[i], x, preferred_element_type=F32)
            y32[pl.ds(i, NLAT, stride=EACH), :] = jnp.where(
                level < LEV, y[0:NLAT], jnp.where(level < 2 * LEV, y[NLAT : 2 * NLAT], y[2 * NLAT :])
            )
        for target in range(N_LEV):
            lanes = slice((target % 2) * SLOT, (target % 2) * SLOT + columns)
            pieces = []
            for r in range(N_LAT):
                t = r * ROWS + target // 2
                pieces.append(y32[t * EACH : (t + 1) * EACH, lanes])
            g1[n][target * EACH : (target + 1) * EACH, :] = jnp.concatenate(pieces, axis=1).astype(BF16)
        z_send(n, 2, g1[n], g2[n])

    def middle_back(n):
        columns = 2 * SIZES[n]
        z_all(n, 2, g1[n], g2[n]).wait_recv()
        for j in range(N_LAT * columns // LANES):
            cols = slice(j * LANES, (j + 1) * LANES)
            mid[cols, :] = g2[n][:, cols].astype(F32).T
        for r in range(N_LAT):
            block = mid[r * columns : (r + 1) * columns, :]
            if padded(columns) > columns:
                block = jnp.concatenate([block, jnp.zeros((padded(columns) - columns, LANES), F32)], axis=0)
            gs[n][r] = block.astype(BF16)
        xy_send(n, 3, gs[n], g3[n])

    def inverse_start(n):
        size, columns = SIZES[n], 2 * SIZES[n]
        xy_all(n, 3, gs[n], g3[n]).wait_recv()
        for w in range(N_LAT):
            ft[0:columns, w * LANES : (w + 1) * LANES] = g3[n][w].astype(F32)[0:columns, :]
        re, im = ft[0:size, :], ft[size:columns, :]
        ur[n][0:size, :] = re
        ui[n][0:size, :] = im
        ur[n][size:columns, :] = re * c1 - im * s1
        ui[n][size:columns, :] = re * s1 + im * c1

    def y_copy(n, target, source):
        return pltpu.make_async_remote_copy(
            src_ref=ys[n].at[target],
            dst_ref=yr[n].at[source],
            send_sem=ys_sem.at[n, target],
            recv_sem=yr_sem.at[n, source],
            device_id=(lat, target),
            device_id_type=MESH,
        )

    def inverse(n, first, last):
        rows = 2 * KK * SIZES[n]
        row = lax.broadcasted_iota(jnp.int32, (rows, K0), 0)
        point = lax.broadcasted_iota(jnp.int32, (rows, K0), 1)
        for kk in range(1, 2 * KK):
            point = point + jnp.where(row >= kk * SIZES[n], K0, 0)

        def step(index, carry):
            chip = chip_at(3 - index)
            total = jnp.zeros((rows, K0), F32)
            for w in range(M // WT):
                cols = slice(w * WT, (w + 1) * WT)
                vr, vi = ur[n][:, cols], ui[n][:, cols]
                tr, ti = [], []
                for k in range(2 * PAIRS):
                    c = twc[pl.ds(chip * (2 * PAIRS) + k, 1), cols]
                    s = tws[pl.ds(chip * (2 * PAIRS) + k, 1), cols]
                    tr.append(vr * c - vi * s)
                    ti.append(vr * s + vi * c)
                total = total + nt_dot(jnp.concatenate(tr, axis=0).astype(BF16), basis[:, cols])
                total = total + nt_dot(
                    jnp.concatenate(ti, axis=0).astype(BF16), basis[:, M + w * WT : M + (w + 1) * WT]
                )
            total = jnp.where(point + chip * (2 * PTS) < count, total, 0.0).astype(BF16)
            for q in range(2):
                p = 2 * chip + q
                ys[n][p] = total[q * (rows // 2) : (q + 1) * (rows // 2)]

                @pl.when(p != lev)
                def _(p=p):
                    y_copy(n, p, lev).start()

            return carry

        lax.fori_loop(first, last, step, 0)

    forward_start(0)
    forward(0, 0, 4)
    forward_end(0)
    forward_start(1)
    forward(1, 0, 1)
    middle(0)
    forward(1, 1, 4)
    forward_end(1)
    apply(0)
    middle(1)
    middle_back(0)
    apply(1)
    inverse_start(0)
    inverse(0, 0, 2)
    middle_back(1)
    inverse(0, 2, 4)
    inverse_start(1)
    inverse(1, 0, 4)

    for n in CHUNKS:
        yr[n][lev] = ys[n][lev]

        def waited(d, carry, n=n):
            y_copy(n, lev, lax.rem(lev + d, N_LEV)).wait_recv()
            return carry

        lax.fori_loop(1, N_LEV, waited, 0)

    def finish_row(t, carry):
        for n in CHUNKS:
            for h in range(2):
                stages[n][h] = yr[n][2 * t + h].astype(F32)
                first = h * HALF + STARTS[n]
                for kk in range(KK):
                    o32[first : first + SIZES[n], kk * K0 : (kk + 1) * K0] = stages[n][
                        h, kk * SIZES[n] : (kk + 1) * SIZES[n], :
                    ]
        out[t] = o32[...].astype(BF16)
        return carry

    lax.fori_loop(0, ROWS, finish_row, 0)

    for n in CHUNKS:

        def sent(d, carry, n=n):
            target = lax.rem(lev + d, N_LEV)
            x_copy(n, target, lev).wait_send()
            y_copy(n, target, lev).wait_send()
            return carry

        lax.fori_loop(1, N_LEV, sent, 0)
        xy_all(n, 0, fs[n], f1[n]).wait_send()
        z_all(n, 1, m1[n], f2[n]).wait_send()
        z_all(n, 2, g1[n], g2[n]).wait_send()
        xy_all(n, 3, gs[n], g3[n]).wait_send()


def body(fields, lat_order, counts, wave_order, weights, diffusion, legendre):
    smem, vmem = pl.BlockSpec(memory_space=pltpu.SMEM), pl.BlockSpec(memory_space=pltpu.VMEM)
    dma = pltpu.SemaphoreType.DMA

    def each(shape, dtype):
        return tuple(pltpu.VMEM(shape(size), dtype) for size in SIZES)

    block = each(lambda size: (N_LEV, KK * size, K0), BF16)
    acc = each(lambda size: (2 * size, M), F32)
    tiles = each(lambda size: (N_LAT, padded(2 * size), LANES), BF16)
    slabs = each(lambda size: (LANES, N_LAT * 2 * size), BF16)
    table = pltpu.VMEM((16, M), F32)
    square = pltpu.VMEM((NLAT, NLAT), F32)
    owned = pltpu.VMEM((NLAT * EACH, LANES), F32)
    return pl.pallas_call(
        kernel,
        out_shape=jax.ShapeDtypeStruct(fields.shape, BF16),
        in_specs=[smem] * 5 + [vmem, vmem, pl.BlockSpec(memory_space=pl.ANY)],
        out_specs=vmem,
        scratch_shapes=[
            pltpu.VMEM((EACH, NLAT, M), F32),
            pltpu.VMEM((2, FL, K0), F32),
            each(lambda size: (2, KK * size, K0), F32),
            block, block,
            pltpu.VMEM((K0, 2 * M), BF16),
            pltpu.VMEM((32, M), F32), pltpu.VMEM((32, M), F32),
            table, table, table, table,
            pltpu.VMEM((2, 8, M), F32),
            acc, acc,
            pltpu.VMEM((padded(2 * max(SIZES)), M), F32),
            tiles, tiles,
            pltpu.VMEM((N_LAT * 2 * max(SIZES), LANES), F32),
            slabs, slabs,
            owned, owned,
            slabs, slabs,
            tiles, tiles,
            square, square, square,
            pltpu.VMEM((3 * NLAT, M), BF16),
            pltpu.VMEM((EACH, 3 * NLAT, NLAT), BF16),
            acc, acc,
            block, block,
            pltpu.VMEM((FL, M), F32),
            dma,
            dma((2, N_LEV)), dma((2, N_LEV)), dma((2, N_LEV)), dma((2, N_LEV)),
            dma((2, 4, 2)),
        ],
        compiler_params=pltpu.CompilerParams(
            collective_id=0, has_side_effects=True, vmem_limit_bytes=56 * 1024 * 1024
        ),
        cost_estimate=pl.CostEstimate(
            flops=20_000_000_000, bytes_accessed=12_000_000, transcendentals=0
        ),
    )(lat_order, counts, wave_order, weights, diffusion, wave_order.reshape(1, M), fields, legendre)


def solution(mesh):
    placed = (P("lat", None, "lev"), P(), P(), P(), P(), P(), P(("lat", "lev"), None, None))
    return jax.shard_map(
        body, mesh=mesh, in_specs=placed, out_specs=P("lat", None, "lev"), check_vma=False
    )
```

```python
import math

import jax
import jax.numpy as jnp
from jax import lax
from jax.experimental import pallas as pl
from jax.experimental.pallas import tpu as pltpu
from jax.sharding import PartitionSpec as P

F32, BF16 = jnp.float32, jnp.bfloat16
MESH = pl.DeviceIdType.MESH

M = 2048
N_LAT, N_LEV = 16, 8
DEV = N_LAT * N_LEV
NLAT = 64
LEV = 24
FL = 72
HALF = FL // 2
ROWS = NLAT // N_LAT
PTS = 2048
K0 = 256
KK = PTS // K0
PAIRS = KK // 2
EACH = M // DEV
WT = 256
LANES = 128
SIZES = (20, 16)
STARTS = (0, 20)
CHUNKS = range(len(SIZES))
SLOT = 64


def padded(rows):
    return -(-rows // 16) * 16


def nt_dot(a, b):
    return lax.dot_general(a, b, (((1,), (1,)), ((), ())), preferred_element_type=F32)


def sincos(wave, factor, count):
    product = wave * factor
    countf = count.astype(F32)
    turns = jnp.floor(product.astype(F32) * (1.0 / countf) + 0.5).astype(jnp.int32)
    rest = product - turns * count
    rest = jnp.where(2 * rest > count, rest - count, rest)
    rest = jnp.where(2 * rest < -count, rest + count, rest)
    z = rest.astype(F32) * (math.pi / countf)
    y = z * z
    s = jnp.full_like(y, 1.0 / math.factorial(13))
    for k in (11, 9, 7, 5, 3, 1):
        s = s * y + (-1.0) ** (k // 2) / math.factorial(k)
    s = s * z
    c = jnp.full_like(y, 1.0 / math.factorial(14) * -1.0)
    for k in (12, 10, 8, 6, 4, 2, 0):
        c = c * y + (-1.0) ** (k // 2) / math.factorial(k)
    return 1.0 - 2.0 * s * s, 2.0 * s * c


def kernel(
    lat_s, cnt_s, wave_s, wgt_s, dif_s, wave_v, fields, leg_hbm, out,
    leg, tmp, stages, xs, xr, basis, twc, tws, ebc, ebs, eac, eas, one,
    accr, acci, ft, fs, f1, mid, m1, f2, x32, y32, g1, g2, gs, g3,
    pm, cn, wt, bs, gst, ur, ui, ys, yr, o32,
    leg_sem, xs_sem, xr_sem, ys_sem, yr_sem, tile_sem,
):
    lat, lev = lax.axis_index("lat"), lax.axis_index("lev")
    z = lev // 2

    barrier = pltpu.get_barrier_semaphore()

    def greet_lev(d, carry):
        pl.semaphore_signal(
            barrier, inc=1, device_id=(lat, lax.rem(lev + d, N_LEV)), device_id_type=MESH
        )
        return carry

    def greet_lat(d, carry):
        pl.semaphore_signal(
            barrier, inc=1, device_id=(lax.rem(lat + d, N_LAT), lev), device_id_type=MESH
        )
        return carry

    lax.fori_loop(1, N_LEV, greet_lev, 0)
    lax.fori_loop(1, N_LAT, greet_lat, 0)
    leg_copy = pltpu.make_async_copy(leg_hbm, leg, leg_sem)
    leg_copy.start()

    lane = lax.broadcasted_iota(jnp.int32, (FL, K0), 1)

    def stage_row(t, carry):
        count = cnt_s[lat_s[ROWS * lat + t]]
        for kk in range(KK):
            x = fields[t, :, kk * K0 : (kk + 1) * K0].astype(F32)
            tmp[kk % 2] = jnp.where(lane + (lev * PTS + kk * K0) < count, x, 0.0)
            for n in CHUNKS:
                for h in range(2):
                    first = h * HALF + STARTS[n]
                    stages[n][h, kk * SIZES[n] : (kk + 1) * SIZES[n], :] = tmp[
                        kk % 2, first : first + SIZES[n], :
                    ]
        for n in CHUNKS:
            for h in range(2):
                xs[n][2 * t + h] = stages[n][h].astype(BF16)
        return carry

    lax.fori_loop(0, ROWS, stage_row, 0)

    pl.semaphore_wait(barrier, N_LEV - 1 + N_LAT - 1)

    def x_copy(n, target, source):
        return pltpu.make_async_remote_copy(
            src_ref=xs[n].at[target],
            dst_ref=xr[n].at[source],
            send_sem=xs_sem.at[n, target],
            recv_sem=xr_sem.at[n, source],
            device_id=(lat, target),
            device_id_type=MESH,
        )

    other = lev + 1 - 2 * lax.rem(lev, 2)

    def partner(step):
        chip_step = step // 2
        far = jnp.where(chip_step == 0, 1, jnp.where(chip_step == 1, 3, 2))
        return 2 * lax.rem(z + far, 4) + lax.rem(lev + lax.rem(step, 2), 2)

    def points_send(n):
        x_copy(n, other, lev).start()

        def send_x(step, carry):
            x_copy(n, partner(step), lev).start()
            return carry

        lax.fori_loop(0, 6, send_x, 0)

    points_send(0)

    count = cnt_s[lat_s[ROWS * lat + z]]
    waves16 = jnp.broadcast_to(wave_v[...], (16, M))
    row16 = lax.broadcasted_iota(jnp.int32, (16, M), 0)
    ebc[...], ebs[...] = sincos(waves16, row16, count)
    eac[...], eas[...] = sincos(waves16, row16 * 16, count)
    twc[0:16], tws[0:16] = sincos(waves16, row16 * (2 * K0), count)
    twc[16:32], tws[16:32] = sincos(waves16, row16 * (2 * K0) + 32 * K0, count)
    waves8 = jnp.broadcast_to(wave_v[...], (8, M))
    one[0], one[1] = sincos(waves8, jnp.full((8, M), K0, jnp.int32), count)

    def basis_rows(a, carry):
        ca, sa = eac[pl.ds(a, 1), :], eas[pl.ds(a, 1), :]
        cb, sb = ebc[...], ebs[...]
        rows = pl.ds(pl.multiple_of(a * 16, 16), 16)
        basis[rows, 0:M] = (ca * cb - sa * sb).astype(BF16)
        basis[rows, M : 2 * M] = (-(sa * cb + ca * sb)).astype(BF16)
        return carry

    lax.fori_loop(0, 16, basis_rows, 0)

    lane64 = lax.broadcasted_iota(jnp.int32, (1, NLAT), 1)

    def slot_row(t, carry):
        j = lat_s[t]
        row = pl.ds(t, 1)
        pm[row, :] = jnp.where(lane64 == j, 1.0, 0.0)
        cn[row, :] = jnp.full((1, NLAT), cnt_s[j], jnp.int32).astype(F32)
        wt[row, :] = jnp.full((1, NLAT), wgt_s[j], F32)
        return carry

    lax.fori_loop(0, NLAT, slot_row, 0)
    eye = lax.broadcasted_iota(jnp.int32, (NLAT, NLAT), 0) == lax.broadcasted_iota(
        jnp.int32, (NLAT, NLAT), 1
    )
    count_col = cn[...]
    count_row = jnp.sum(jnp.where(eye, count_col, 0.0), axis=0, keepdims=True)
    share_row = jnp.sum(jnp.where(eye, wt[...], 0.0), axis=0, keepdims=True) / count_row
    perm = pm[...].astype(BF16)
    degree = lax.broadcasted_iota(jnp.int32, (1, M), 1)
    leg_copy.wait()

    def operator(i, carry):
        m = wave_s[(lat * N_LEV + lev) * EACH + i]
        deg = (degree + m).astype(F32)
        scaled = deg * (deg + 1.0) * (1.0 / float(M * (M - 1)))
        scaled = scaled * scaled
        own = jnp.dot(perm, leg[i].astype(BF16), preferred_element_type=F32)
        for f in range(3):
            bs[f * NLAT : (f + 1) * NLAT, :] = (own * (1.0 / (1.0 + dif_s[f] * scaled))).astype(BF16)
        g = nt_dot(bs[...], own.astype(BF16))
        twice_m = (2 * jnp.full((1, NLAT), m, jnp.int32)).astype(F32)
        from_row = jnp.where(twice_m < count_row, share_row, 0.0)
        to_col = jnp.where(twice_m < count_col, jnp.where(twice_m == 0.0, 1.0, 2.0), 0.0)
        scale = to_col * from_row
        for f in range(3):
            gst[i, f * NLAT : (f + 1) * NLAT, :] = (g[f * NLAT : (f + 1) * NLAT, :] * scale).astype(BF16)
        return carry

    def operators(first, last):
        lax.fori_loop(first, last, operator, 0)

    x32[...] = jnp.zeros_like(x32)
    ft[...] = jnp.zeros_like(ft)
    c1, s1 = one[0, 0:1, :], one[1, 0:1, :]

    def xy_copy(n, k, source, target_ref, d):
        target = lax.rem(lat + d, N_LAT)
        return pltpu.make_async_remote_copy(
            src_ref=source.at[target],
            dst_ref=target_ref.at[lat],
            send_sem=tile_sem.at[n, k, 0],
            recv_sem=tile_sem.at[n, k, 1],
            device_id=(target, lev),
            device_id_type=MESH,
        )

    def xy_send(n, k, source, target_ref):
        def step(d, carry):
            xy_copy(n, k, source, target_ref, d).start()
            return carry

        lax.fori_loop(1, N_LAT, step, 0)
        target_ref[lat] = source[lat]

    def xy_all(n, k, source, target_ref):
        return pltpu.make_async_remote_copy(
            src_ref=source.at[pl.ds(0, N_LAT - 1)],
            dst_ref=target_ref.at[pl.ds(0, N_LAT - 1)],
            send_sem=tile_sem.at[n, k, 0],
            recv_sem=tile_sem.at[n, k, 1],
            device_id=(lax.rem(lat + 1, N_LAT), lev),
            device_id_type=MESH,
        )

    def slab(index):
        return pl.ds(pl.multiple_of(index * EACH, EACH), EACH)

    def z_send(n, k, source, target_ref):
        def step(d, carry):
            target = lax.rem(lev + d, N_LEV)
            pltpu.make_async_remote_copy(
                src_ref=source.at[slab(target), :],
                dst_ref=target_ref.at[slab(lev), :],
                send_sem=tile_sem.at[n, k, 0],
                recv_sem=tile_sem.at[n, k, 1],
                device_id=(lat, target),
                device_id_type=MESH,
            ).start()
            return carry

        lax.fori_loop(1, N_LEV, step, 0)
        target_ref[slab(lev), :] = source[slab(lev), :]

    def z_all(n, k, source, target_ref):
        whole = pl.ds(0, (N_LEV - 1) * EACH)
        return pltpu.make_async_remote_copy(
            src_ref=source.at[whole, :],
            dst_ref=target_ref.at[whole, :],
            send_sem=tile_sem.at[n, k, 0],
            recv_sem=tile_sem.at[n, k, 1],
            device_id=(lat, lax.rem(lev + 1, N_LEV)),
            device_id_type=MESH,
        )

    def chip_at(step):
        far = jnp.where(step == 0, 0, jnp.where(step == 1, 3, jnp.where(step == 2, 1, 2)))
        return lax.rem(z + far, 4)

    def forward_start(n):
        accr[n][...] = jnp.zeros_like(accr[n])
        acci[n][...] = jnp.zeros_like(acci[n])
        xr[n][lev] = xs[n][lev]

    def forward(n, first, last):
        columns = 2 * SIZES[n]

        def step(index, carry):
            chip = chip_at(index)
            for q in range(2):
                p = 2 * chip + q

                @pl.when(p != lev)
                def _(p=p):
                    x_copy(n, p, p).wait_recv()

            points = xr[n][pl.ds(2 * chip, 2)].reshape(2 * KK * SIZES[n], K0)
            for w in range(M // WT):
                cols = slice(w * WT, (w + 1) * WT)
                pr = jnp.dot(points, basis[:, cols], preferred_element_type=F32)
                pi = jnp.dot(points, basis[:, M + w * WT : M + (w + 1) * WT], preferred_element_type=F32)
                ar, ai = accr[n][:, cols], acci[n][:, cols]
                for k in range(2 * PAIRS):
                    c = twc[pl.ds(chip * (2 * PAIRS) + k, 1), cols]
                    s = tws[pl.ds(chip * (2 * PAIRS) + k, 1), cols]
                    br, bi = pr[k * columns : (k + 1) * columns], pi[k * columns : (k + 1) * columns]
                    ar = ar + (br * c + bi * s)
                    ai = ai + (bi * c - br * s)
                accr[n][:, cols] = ar
                acci[n][:, cols] = ai
            return carry

        lax.fori_loop(first, last, step, 0)

    def forward_end(n):
        size, columns = SIZES[n], 2 * SIZES[n]
        odd_r, odd_i = accr[n][size:columns, :], acci[n][size:columns, :]
        ft[0:size, :] = accr[n][0:size, :] + (odd_r * c1 + odd_i * s1)
        ft[size:columns, :] = acci[n][0:size, :] + (odd_i * c1 - odd_r * s1)
        for w in range(N_LAT):
            fs[n][w] = ft[0 : padded(columns), w * LANES : (w + 1) * LANES].astype(BF16)
        xy_send(n, 0, fs[n], f1[n])

    def middle(n):
        columns = 2 * SIZES[n]
        xy_all(n, 0, fs[n], f1[n]).wait_recv()
        for r in range(N_LAT):
            mid[r * columns : (r + 1) * columns, :] = f1[n][r].astype(F32)[0:columns, :]
        for j in range(N_LAT * columns // LANES):
            cols = slice(j * LANES, (j + 1) * LANES)
            m1[n][:, cols] = mid[cols, :].T.astype(BF16)
        z_send(n, 1, m1[n], f2[n])

    def apply(n):
        size, columns = SIZES[n], 2 * SIZES[n]
        z_all(n, 1, m1[n], f2[n]).wait_recv()
        for source in range(N_LEV):
            v = f2[n][source * EACH : (source + 1) * EACH, :].astype(F32)
            lanes = slice((source % 2) * SLOT, (source % 2) * SLOT + columns)
            for r in range(N_LAT):
                t = r * ROWS + source // 2
                x32[t * EACH : (t + 1) * EACH, lanes] = v[:, r * columns : (r + 1) * columns]
        column = lax.broadcasted_iota(jnp.int32, (NLAT, LANES), 1)
        level = STARTS[n] + jnp.where(column >= SLOT, column - SLOT + HALF, column)
        inside = jnp.where(column >= SLOT, column - SLOT, column)
        level = jnp.where(inside >= size, level - size, level)
        for i in range(EACH):
            x = x32[pl.ds(i, NLAT, stride=EACH), :].astype(BF16)
            y = jnp.dot(gst[i], x, preferred_element_type=F32)
            y32[pl.ds(i, NLAT, stride=EACH), :] = jnp.where(
                level < LEV, y[0:NLAT], jnp.where(level < 2 * LEV, y[NLAT : 2 * NLAT], y[2 * NLAT :])
            )
        for target in range(N_LEV):
            lanes = slice((target % 2) * SLOT, (target % 2) * SLOT + columns)
            pieces = []
            for r in range(N_LAT):
                t = r * ROWS + target // 2
                pieces.append(y32[t * EACH : (t + 1) * EACH, lanes])
            g1[n][target * EACH : (target + 1) * EACH, :] = jnp.concatenate(pieces, axis=1).astype(BF16)
        z_send(n, 2, g1[n], g2[n])

    def middle_back(n):
        columns = 2 * SIZES[n]
        z_all(n, 2, g1[n], g2[n]).wait_recv()
        for j in range(N_LAT * columns // LANES):
            cols = slice(j * LANES, (j + 1) * LANES)
            mid[cols, :] = g2[n][:, cols].astype(F32).T
        for r in range(N_LAT):
            block = mid[r * columns : (r + 1) * columns, :]
            if padded(columns) > columns:
                block = jnp.concatenate([block, jnp.zeros((padded(columns) - columns, LANES), F32)], axis=0)
            gs[n][r] = block.astype(BF16)
        xy_send(n, 3, gs[n], g3[n])

    def inverse_start(n):
        size, columns = SIZES[n], 2 * SIZES[n]
        xy_all(n, 3, gs[n], g3[n]).wait_recv()
        for w in range(N_LAT):
            ft[0:columns, w * LANES : (w + 1) * LANES] = g3[n][w].astype(F32)[0:columns, :]
        re, im = ft[0:size, :], ft[size:columns, :]
        ur[n][0:size, :] = re
        ui[n][0:size, :] = im
        ur[n][size:columns, :] = re * c1 - im * s1
        ui[n][size:columns, :] = re * s1 + im * c1

    def y_copy(n, target, source):
        return pltpu.make_async_remote_copy(
            src_ref=ys[n].at[target],
            dst_ref=yr[n].at[source],
            send_sem=ys_sem.at[n, target],
            recv_sem=yr_sem.at[n, source],
            device_id=(lat, target),
            device_id_type=MESH,
        )

    def inverse(n, first, last):
        rows = 2 * KK * SIZES[n]
        row = lax.broadcasted_iota(jnp.int32, (rows, K0), 0)
        point = lax.broadcasted_iota(jnp.int32, (rows, K0), 1)
        for kk in range(1, 2 * KK):
            point = point + jnp.where(row >= kk * SIZES[n], K0, 0)

        def step(index, carry):
            chip = chip_at(3 - index)
            total = jnp.zeros((rows, K0), F32)
            for w in range(M // WT):
                cols = slice(w * WT, (w + 1) * WT)
                vr, vi = ur[n][:, cols], ui[n][:, cols]
                tr, ti = [], []
                for k in range(2 * PAIRS):
                    c = twc[pl.ds(chip * (2 * PAIRS) + k, 1), cols]
                    s = tws[pl.ds(chip * (2 * PAIRS) + k, 1), cols]
                    tr.append(vr * c - vi * s)
                    ti.append(vr * s + vi * c)
                total = total + nt_dot(jnp.concatenate(tr, axis=0).astype(BF16), basis[:, cols])
                total = total + nt_dot(
                    jnp.concatenate(ti, axis=0).astype(BF16), basis[:, M + w * WT : M + (w + 1) * WT]
                )
            total = jnp.where(point + chip * (2 * PTS) < count, total, 0.0).astype(BF16)
            for q in range(2):
                p = 2 * chip + q
                ys[n][p] = total[q * (rows // 2) : (q + 1) * (rows // 2)]

                @pl.when(p != lev)
                def _(p=p):
                    y_copy(n, p, lev).start()

            return carry

        lax.fori_loop(first, last, step, 0)

    operators(0, 8)
    points_send(1)
    forward_start(0)
    forward(0, 0, 4)
    forward_end(0)
    operators(8, 16)
    forward_start(1)
    forward(1, 0, 1)
    middle(0)
    forward(1, 1, 4)
    forward_end(1)
    apply(0)
    middle(1)
    middle_back(0)
    apply(1)
    inverse_start(0)
    inverse(0, 0, 2)
    middle_back(1)
    inverse(0, 2, 4)
    inverse_start(1)
    inverse(1, 0, 4)

    for n in CHUNKS:
        yr[n][lev] = ys[n][lev]

        def waited(d, carry, n=n):
            y_copy(n, lev, lax.rem(lev + d, N_LEV)).wait_recv()
            return carry

        lax.fori_loop(1, N_LEV, waited, 0)

    def finish_row(t, carry):
        for n in CHUNKS:
            for h in range(2):
                stages[n][h] = yr[n][2 * t + h].astype(F32)
                first = h * HALF + STARTS[n]
                for kk in range(KK):
                    o32[first : first + SIZES[n], kk * K0 : (kk + 1) * K0] = stages[n][
                        h, kk * SIZES[n] : (kk + 1) * SIZES[n], :
                    ]
        out[t] = o32[...].astype(BF16)
        return carry

    lax.fori_loop(0, ROWS, finish_row, 0)

    for n in CHUNKS:

        def sent(d, carry, n=n):
            target = lax.rem(lev + d, N_LEV)
            x_copy(n, target, lev).wait_send()
            y_copy(n, target, lev).wait_send()
            return carry

        lax.fori_loop(1, N_LEV, sent, 0)
        xy_all(n, 0, fs[n], f1[n]).wait_send()
        z_all(n, 1, m1[n], f2[n]).wait_send()
        z_all(n, 2, g1[n], g2[n]).wait_send()
        xy_all(n, 3, gs[n], g3[n]).wait_send()


def body(fields, lat_order, counts, wave_order, weights, diffusion, legendre):
    smem, vmem = pl.BlockSpec(memory_space=pltpu.SMEM), pl.BlockSpec(memory_space=pltpu.VMEM)
    dma = pltpu.SemaphoreType.DMA

    def each(shape, dtype):
        return tuple(pltpu.VMEM(shape(size), dtype) for size in SIZES)

    block = each(lambda size: (N_LEV, KK * size, K0), BF16)
    acc = each(lambda size: (2 * size, M), F32)
    tiles = each(lambda size: (N_LAT, padded(2 * size), LANES), BF16)
    slabs = each(lambda size: (LANES, N_LAT * 2 * size), BF16)
    table = pltpu.VMEM((16, M), F32)
    square = pltpu.VMEM((NLAT, NLAT), F32)
    owned = pltpu.VMEM((NLAT * EACH, LANES), F32)
    return pl.pallas_call(
        kernel,
        out_shape=jax.ShapeDtypeStruct(fields.shape, BF16),
        in_specs=[smem] * 5 + [vmem, vmem, pl.BlockSpec(memory_space=pl.ANY)],
        out_specs=vmem,
        scratch_shapes=[
            pltpu.VMEM((EACH, NLAT, M), F32),
            pltpu.VMEM((2, FL, K0), F32),
            each(lambda size: (2, KK * size, K0), F32),
            block, block,
            pltpu.VMEM((K0, 2 * M), BF16),
            pltpu.VMEM((32, M), F32), pltpu.VMEM((32, M), F32),
            table, table, table, table,
            pltpu.VMEM((2, 8, M), F32),
            acc, acc,
            pltpu.VMEM((padded(2 * max(SIZES)), M), F32),
            tiles, tiles,
            pltpu.VMEM((N_LAT * 2 * max(SIZES), LANES), F32),
            slabs, slabs,
            owned, owned,
            slabs, slabs,
            tiles, tiles,
            square, square, square,
            pltpu.VMEM((3 * NLAT, M), BF16),
            pltpu.VMEM((EACH, 3 * NLAT, NLAT), BF16),
            acc, acc,
            block, block,
            pltpu.VMEM((FL, M), F32),
            dma,
            dma((2, N_LEV)), dma((2, N_LEV)), dma((2, N_LEV)), dma((2, N_LEV)),
            dma((2, 4, 2)),
        ],
        compiler_params=pltpu.CompilerParams(
            collective_id=0, has_side_effects=True, vmem_limit_bytes=56 * 1024 * 1024
        ),
        cost_estimate=pl.CostEstimate(
            flops=20_000_000_000, bytes_accessed=12_000_000, transcendentals=0
        ),
    )(lat_order, counts, wave_order, weights, diffusion, wave_order.reshape(1, M), fields, legendre)


def solution(mesh):
    placed = (P("lat", None, "lev"), P(), P(), P(), P(), P(), P(("lat", "lev"), None, None))
    return jax.shard_map(
        body, mesh=mesh, in_specs=placed, out_specs=P("lat", None, "lev"), check_vma=False
    )
```

```python
import math

import jax
import jax.numpy as jnp
from jax import lax
from jax.experimental import pallas as pl
from jax.experimental.pallas import tpu as pltpu
from jax.sharding import PartitionSpec as P

F32, BF16 = jnp.float32, jnp.bfloat16
MESH = pl.DeviceIdType.MESH

M = 2048
N_LAT, N_LEV = 16, 8
DEV = N_LAT * N_LEV
NLAT = 64
LEV = 24
FL = 72
HALF = FL // 2
ROWS = NLAT // N_LAT
PTS = 2048
K0 = 256
KK = PTS // K0
PAIRS = KK // 2
EACH = M // DEV
WT = 256
LANES = 128
SIZES = (20, 16)
STARTS = (0, 20)
CHUNKS = range(len(SIZES))
SLOT = 64


def padded(rows):
    return -(-rows // 16) * 16


def nt_dot(a, b):
    return lax.dot_general(a, b, (((1,), (1,)), ((), ())), preferred_element_type=F32)


def sincos(wave, factor, count):
    product = wave * factor
    countf = count.astype(F32)
    turns = jnp.floor(product.astype(F32) * (1.0 / countf) + 0.5).astype(jnp.int32)
    rest = product - turns * count
    rest = jnp.where(2 * rest > count, rest - count, rest)
    rest = jnp.where(2 * rest < -count, rest + count, rest)
    z = rest.astype(F32) * (math.pi / countf)
    y = z * z
    s = jnp.full_like(y, 1.0 / math.factorial(13))
    for k in (11, 9, 7, 5, 3, 1):
        s = s * y + (-1.0) ** (k // 2) / math.factorial(k)
    s = s * z
    c = jnp.full_like(y, 1.0 / math.factorial(14) * -1.0)
    for k in (12, 10, 8, 6, 4, 2, 0):
        c = c * y + (-1.0) ** (k // 2) / math.factorial(k)
    return 1.0 - 2.0 * s * s, 2.0 * s * c


def kernel(
    lat_s, cnt_s, wave_s, wgt_s, dif_s, wave_v, fields, leg_hbm, out,
    leg, tmp, stages, xs, xr, basis, twc, tws, ebc, ebs, eac, eas, one,
    accr, acci, ft, fs, f1, mid, m1, f2, x32, y32, g1, g2, gs, g3,
    pm, cn, wt, bs, gst, ur, ui, ys, yr, o32,
    leg_sem, xs_sem, xr_sem, ys_sem, yr_sem, tile_sem,
):
    lat, lev = lax.axis_index("lat"), lax.axis_index("lev")
    z = lev // 2

    barrier = pltpu.get_barrier_semaphore()

    def greet_lev(d, carry):
        pl.semaphore_signal(
            barrier, inc=1, device_id=(lat, lax.rem(lev + d, N_LEV)), device_id_type=MESH
        )
        return carry

    def greet_lat(d, carry):
        pl.semaphore_signal(
            barrier, inc=1, device_id=(lax.rem(lat + d, N_LAT), lev), device_id_type=MESH
        )
        return carry

    lax.fori_loop(1, N_LEV, greet_lev, 0)
    lax.fori_loop(1, N_LAT, greet_lat, 0)
    leg_copy = pltpu.make_async_copy(leg_hbm, leg, leg_sem)
    leg_copy.start()

    lane = lax.broadcasted_iota(jnp.int32, (FL, K0), 1)

    def stage_row(t, carry):
        count = cnt_s[lat_s[ROWS * lat + t]]
        for kk in range(KK):
            x = fields[t, :, kk * K0 : (kk + 1) * K0].astype(F32)
            tmp[kk % 2] = jnp.where(lane + (lev * PTS + kk * K0) < count, x, 0.0)
            for n in CHUNKS:
                for h in range(2):
                    first = h * HALF + STARTS[n]
                    stages[n][h, kk * SIZES[n] : (kk + 1) * SIZES[n], :] = tmp[
                        kk % 2, first : first + SIZES[n], :
                    ]
        for n in CHUNKS:
            for h in range(2):
                xs[n][2 * t + h] = stages[n][h].astype(BF16)
        return carry

    lax.fori_loop(0, ROWS, stage_row, 0)

    pl.semaphore_wait(barrier, N_LEV - 1 + N_LAT - 1)

    def x_copy(n, target, source):
        return pltpu.make_async_remote_copy(
            src_ref=xs[n].at[target],
            dst_ref=xr[n].at[source],
            send_sem=xs_sem.at[n, target],
            recv_sem=xr_sem.at[n, source],
            device_id=(lat, target),
            device_id_type=MESH,
        )

    other = lev + 1 - 2 * lax.rem(lev, 2)

    def partner(step):
        chip_step = step // 2
        far = jnp.where(chip_step == 0, 1, jnp.where(chip_step == 1, 3, 2))
        return 2 * lax.rem(z + far, 4) + lax.rem(lev + lax.rem(step, 2), 2)

    def points_send(n):
        x_copy(n, other, lev).start()

        def send_x(step, carry):
            x_copy(n, partner(step), lev).start()
            return carry

        lax.fori_loop(0, 6, send_x, 0)

    points_send(0)

    count = cnt_s[lat_s[ROWS * lat + z]]
    waves16 = jnp.broadcast_to(wave_v[...], (16, M))
    row16 = lax.broadcasted_iota(jnp.int32, (16, M), 0)
    ebc[...], ebs[...] = sincos(waves16, row16, count)
    eac[...], eas[...] = sincos(waves16, row16 * 16, count)
    twc[0:16], tws[0:16] = sincos(waves16, row16 * (2 * K0), count)
    twc[16:32], tws[16:32] = sincos(waves16, row16 * (2 * K0) + 32 * K0, count)
    waves8 = jnp.broadcast_to(wave_v[...], (8, M))
    one[0], one[1] = sincos(waves8, jnp.full((8, M), K0, jnp.int32), count)

    def basis_rows(a, carry):
        ca, sa = eac[pl.ds(a, 1), :], eas[pl.ds(a, 1), :]
        cb, sb = ebc[...], ebs[...]
        rows = pl.ds(pl.multiple_of(a * 16, 16), 16)
        basis[rows, 0:M] = (ca * cb - sa * sb).astype(BF16)
        basis[rows, M : 2 * M] = (-(sa * cb + ca * sb)).astype(BF16)
        return carry

    lax.fori_loop(0, 16, basis_rows, 0)

    lane64 = lax.broadcasted_iota(jnp.int32, (1, NLAT), 1)

    def slot_row(t, carry):
        j = lat_s[t]
        row = pl.ds(t, 1)
        pm[row, :] = jnp.where(lane64 == j, 1.0, 0.0)
        cn[row, :] = jnp.full((1, NLAT), cnt_s[j], jnp.int32).astype(F32)
        wt[row, :] = jnp.full((1, NLAT), wgt_s[j], F32)
        return carry

    lax.fori_loop(0, NLAT, slot_row, 0)
    eye = lax.broadcasted_iota(jnp.int32, (NLAT, NLAT), 0) == lax.broadcasted_iota(
        jnp.int32, (NLAT, NLAT), 1
    )
    count_col = cn[...]
    count_row = jnp.sum(jnp.where(eye, count_col, 0.0), axis=0, keepdims=True)
    share_row = jnp.sum(jnp.where(eye, wt[...], 0.0), axis=0, keepdims=True) / count_row
    perm = pm[...].astype(BF16)
    degree = lax.broadcasted_iota(jnp.int32, (1, M), 1)
    leg_copy.wait()

    def operator(i, carry):
        m = wave_s[(lat * N_LEV + lev) * EACH + i]
        deg = (degree + m).astype(F32)
        scaled = deg * (deg + 1.0) * (1.0 / float(M * (M - 1)))
        scaled = scaled * scaled
        own = jnp.dot(perm, leg[i].astype(BF16), preferred_element_type=F32)
        for f in range(3):
            bs[f * NLAT : (f + 1) * NLAT, :] = (own * (1.0 / (1.0 + dif_s[f] * scaled))).astype(BF16)
        g = nt_dot(bs[...], own.astype(BF16))
        twice_m = (2 * jnp.full((1, NLAT), m, jnp.int32)).astype(F32)
        from_row = jnp.where(twice_m < count_row, share_row, 0.0)
        to_col = jnp.where(twice_m < count_col, jnp.where(twice_m == 0.0, 1.0, 2.0), 0.0)
        scale = to_col * from_row
        for f in range(3):
            gst[i, f * NLAT : (f + 1) * NLAT, :] = (g[f * NLAT : (f + 1) * NLAT, :] * scale).astype(BF16)
        return carry

    def operators(first, last):
        lax.fori_loop(first, last, operator, 0)

    x32[...] = jnp.zeros_like(x32)
    ft[...] = jnp.zeros_like(ft)
    c1, s1 = one[0, 0:1, :], one[1, 0:1, :]

    def xy_copy(n, k, source, target_ref, d):
        target = lax.rem(lat + d, N_LAT)
        return pltpu.make_async_remote_copy(
            src_ref=source.at[target],
            dst_ref=target_ref.at[lat],
            send_sem=tile_sem.at[n, k, 0],
            recv_sem=tile_sem.at[n, k, 1],
            device_id=(target, lev),
            device_id_type=MESH,
        )

    def xy_send(n, k, source, target_ref):
        def step(d, carry):
            xy_copy(n, k, source, target_ref, d).start()
            return carry

        lax.fori_loop(1, N_LAT, step, 0)
        target_ref[lat] = source[lat]

    def xy_all(n, k, source, target_ref):
        return pltpu.make_async_remote_copy(
            src_ref=source.at[pl.ds(0, N_LAT - 1)],
            dst_ref=target_ref.at[pl.ds(0, N_LAT - 1)],
            send_sem=tile_sem.at[n, k, 0],
            recv_sem=tile_sem.at[n, k, 1],
            device_id=(lax.rem(lat + 1, N_LAT), lev),
            device_id_type=MESH,
        )

    def slab(index):
        return pl.ds(pl.multiple_of(index * EACH, EACH), EACH)

    def z_send(n, k, source, target_ref):
        def step(d, carry):
            target = lax.rem(lev + d, N_LEV)
            pltpu.make_async_remote_copy(
                src_ref=source.at[slab(target), :],
                dst_ref=target_ref.at[slab(lev), :],
                send_sem=tile_sem.at[n, k, 0],
                recv_sem=tile_sem.at[n, k, 1],
                device_id=(lat, target),
                device_id_type=MESH,
            ).start()
            return carry

        lax.fori_loop(1, N_LEV, step, 0)
        target_ref[slab(lev), :] = source[slab(lev), :]

    def z_all(n, k, source, target_ref):
        whole = pl.ds(0, (N_LEV - 1) * EACH)
        return pltpu.make_async_remote_copy(
            src_ref=source.at[whole, :],
            dst_ref=target_ref.at[whole, :],
            send_sem=tile_sem.at[n, k, 0],
            recv_sem=tile_sem.at[n, k, 1],
            device_id=(lat, lax.rem(lev + 1, N_LEV)),
            device_id_type=MESH,
        )

    def chip_at(step):
        far = jnp.where(step == 0, 0, jnp.where(step == 1, 3, jnp.where(step == 2, 1, 2)))
        return lax.rem(z + far, 4)

    def forward_start(n):
        accr[n][...] = jnp.zeros_like(accr[n])
        acci[n][...] = jnp.zeros_like(acci[n])
        xr[n][lev] = xs[n][lev]

    def forward(n, first, last):
        columns = 2 * SIZES[n]

        def step(index, carry):
            chip = chip_at(index)
            for q in range(2):
                p = 2 * chip + q

                @pl.when(p != lev)
                def _(p=p):
                    x_copy(n, p, p).wait_recv()

            points = xr[n][pl.ds(2 * chip, 2)].reshape(2 * KK * SIZES[n], K0)
            for w in range(M // WT):
                cols = slice(w * WT, (w + 1) * WT)
                pr = jnp.dot(points, basis[:, cols], preferred_element_type=F32)
                pi = jnp.dot(points, basis[:, M + w * WT : M + (w + 1) * WT], preferred_element_type=F32)
                ar, ai = accr[n][:, cols], acci[n][:, cols]
                for k in range(2 * PAIRS):
                    c = twc[pl.ds(chip * (2 * PAIRS) + k, 1), cols]
                    s = tws[pl.ds(chip * (2 * PAIRS) + k, 1), cols]
                    br, bi = pr[k * columns : (k + 1) * columns], pi[k * columns : (k + 1) * columns]
                    ar = ar + (br * c + bi * s)
                    ai = ai + (bi * c - br * s)
                accr[n][:, cols] = ar
                acci[n][:, cols] = ai
            return carry

        lax.fori_loop(first, last, step, 0)

    def forward_end(n):
        size, columns = SIZES[n], 2 * SIZES[n]
        odd_r, odd_i = accr[n][size:columns, :], acci[n][size:columns, :]
        ft[0:size, :] = accr[n][0:size, :] + (odd_r * c1 + odd_i * s1)
        ft[size:columns, :] = acci[n][0:size, :] + (odd_i * c1 - odd_r * s1)
        for w in range(N_LAT):
            fs[n][w] = ft[0 : padded(columns), w * LANES : (w + 1) * LANES].astype(BF16)
        xy_send(n, 0, fs[n], f1[n])

    def middle(n):
        columns = 2 * SIZES[n]
        xy_all(n, 0, fs[n], f1[n]).wait_recv()
        for r in range(N_LAT):
            mid[r * columns : (r + 1) * columns, :] = f1[n][r].astype(F32)[0:columns, :]
        for j in range(N_LAT * columns // LANES):
            cols = slice(j * LANES, (j + 1) * LANES)
            m1[n][:, cols] = mid[cols, :].T.astype(BF16)
        z_send(n, 1, m1[n], f2[n])

    def apply(n):
        size, columns = SIZES[n], 2 * SIZES[n]
        z_all(n, 1, m1[n], f2[n]).wait_recv()
        for source in range(N_LEV):
            v = f2[n][source * EACH : (source + 1) * EACH, :].astype(F32)
            lanes = slice((source % 2) * SLOT, (source % 2) * SLOT + columns)
            for r in range(N_LAT):
                t = r * ROWS + source // 2
                x32[t * EACH : (t + 1) * EACH, lanes] = v[:, r * columns : (r + 1) * columns]
        column = lax.broadcasted_iota(jnp.int32, (NLAT, LANES), 1)
        level = STARTS[n] + jnp.where(column >= SLOT, column - SLOT + HALF, column)
        inside = jnp.where(column >= SLOT, column - SLOT, column)
        level = jnp.where(inside >= size, level - size, level)
        for i in range(EACH):
            x = x32[pl.ds(i, NLAT, stride=EACH), :].astype(BF16)
            y = jnp.dot(gst[i], x, preferred_element_type=F32)
            y32[pl.ds(i, NLAT, stride=EACH), :] = jnp.where(
                level < LEV, y[0:NLAT], jnp.where(level < 2 * LEV, y[NLAT : 2 * NLAT], y[2 * NLAT :])
            )
        for target in range(N_LEV):
            lanes = slice((target % 2) * SLOT, (target % 2) * SLOT + columns)
            pieces = []
            for r in range(N_LAT):
                t = r * ROWS + target // 2
                pieces.append(y32[t * EACH : (t + 1) * EACH, lanes])
            g1[n][target * EACH : (target + 1) * EACH, :] = jnp.concatenate(pieces, axis=1).astype(BF16)
        z_send(n, 2, g1[n], g2[n])

    def middle_back(n):
        columns = 2 * SIZES[n]
        z_all(n, 2, g1[n], g2[n]).wait_recv()
        for j in range(N_LAT * columns // LANES):
            cols = slice(j * LANES, (j + 1) * LANES)
            mid[cols, :] = g2[n][:, cols].astype(F32).T
        for r in range(N_LAT):
            block = mid[r * columns : (r + 1) * columns, :]
            if padded(columns) > columns:
                block = jnp.concatenate([block, jnp.zeros((padded(columns) - columns, LANES), F32)], axis=0)
            gs[n][r] = block.astype(BF16)
        xy_send(n, 3, gs[n], g3[n])

    def inverse_start(n):
        size, columns = SIZES[n], 2 * SIZES[n]
        xy_all(n, 3, gs[n], g3[n]).wait_recv()
        for w in range(N_LAT):
            ft[0:columns, w * LANES : (w + 1) * LANES] = g3[n][w].astype(F32)[0:columns, :]
        re, im = ft[0:size, :], ft[size:columns, :]
        ur[n][0:size, :] = re
        ui[n][0:size, :] = im
        ur[n][size:columns, :] = re * c1 - im * s1
        ui[n][size:columns, :] = re * s1 + im * c1

    def y_copy(n, target, source):
        return pltpu.make_async_remote_copy(
            src_ref=ys[n].at[target],
            dst_ref=yr[n].at[source],
            send_sem=ys_sem.at[n, target],
            recv_sem=yr_sem.at[n, source],
            device_id=(lat, target),
            device_id_type=MESH,
        )

    def inverse(n, first, last):
        rows = 2 * KK * SIZES[n]
        row = lax.broadcasted_iota(jnp.int32, (rows, K0), 0)
        point = lax.broadcasted_iota(jnp.int32, (rows, K0), 1)
        for kk in range(1, 2 * KK):
            point = point + jnp.where(row >= kk * SIZES[n], K0, 0)

        def step(index, carry):
            chip = chip_at(3 - index)
            total = jnp.zeros((rows, K0), F32)
            for w in range(M // WT):
                cols = slice(w * WT, (w + 1) * WT)
                vr, vi = ur[n][:, cols], ui[n][:, cols]
                tr, ti = [], []
                for k in range(2 * PAIRS):
                    c = twc[pl.ds(chip * (2 * PAIRS) + k, 1), cols]
                    s = tws[pl.ds(chip * (2 * PAIRS) + k, 1), cols]
                    tr.append(vr * c - vi * s)
                    ti.append(vr * s + vi * c)
                total = total + nt_dot(jnp.concatenate(tr, axis=0).astype(BF16), basis[:, cols])
                total = total + nt_dot(
                    jnp.concatenate(ti, axis=0).astype(BF16), basis[:, M + w * WT : M + (w + 1) * WT]
                )
            total = jnp.where(point + chip * (2 * PTS) < count, total, 0.0).astype(BF16)
            for q in range(2):
                p = 2 * chip + q
                ys[n][p] = total[q * (rows // 2) : (q + 1) * (rows // 2)]

                @pl.when(p != lev)
                def _(p=p):
                    y_copy(n, p, lev).start()

            return carry

        lax.fori_loop(first, last, step, 0)

    operators(0, 8)
    points_send(1)
    forward_start(0)
    forward(0, 0, 4)
    forward_end(0)
    operators(8, 16)
    middle(0)
    forward_start(1)
    forward(1, 0, 4)
    forward_end(1)
    apply(0)
    middle(1)
    middle_back(0)
    apply(1)
    inverse_start(0)
    inverse(0, 0, 2)
    middle_back(1)
    inverse(0, 2, 4)
    inverse_start(1)
    inverse(1, 0, 4)

    for n in CHUNKS:
        yr[n][lev] = ys[n][lev]

        def waited(d, carry, n=n):
            y_copy(n, lev, lax.rem(lev + d, N_LEV)).wait_recv()
            return carry

        lax.fori_loop(1, N_LEV, waited, 0)

    def finish_row(t, carry):
        for n in CHUNKS:
            for h in range(2):
                stages[n][h] = yr[n][2 * t + h].astype(F32)
                first = h * HALF + STARTS[n]
                for kk in range(KK):
                    o32[first : first + SIZES[n], kk * K0 : (kk + 1) * K0] = stages[n][
                        h, kk * SIZES[n] : (kk + 1) * SIZES[n], :
                    ]
        out[t] = o32[...].astype(BF16)
        return carry

    lax.fori_loop(0, ROWS, finish_row, 0)

    for n in CHUNKS:

        def sent(d, carry, n=n):
            target = lax.rem(lev + d, N_LEV)
            x_copy(n, target, lev).wait_send()
            y_copy(n, target, lev).wait_send()
            return carry

        lax.fori_loop(1, N_LEV, sent, 0)
        xy_all(n, 0, fs[n], f1[n]).wait_send()
        z_all(n, 1, m1[n], f2[n]).wait_send()
        z_all(n, 2, g1[n], g2[n]).wait_send()
        xy_all(n, 3, gs[n], g3[n]).wait_send()


def body(fields, lat_order, counts, wave_order, weights, diffusion, legendre):
    smem, vmem = pl.BlockSpec(memory_space=pltpu.SMEM), pl.BlockSpec(memory_space=pltpu.VMEM)
    dma = pltpu.SemaphoreType.DMA

    def each(shape, dtype):
        return tuple(pltpu.VMEM(shape(size), dtype) for size in SIZES)

    block = each(lambda size: (N_LEV, KK * size, K0), BF16)
    acc = each(lambda size: (2 * size, M), F32)
    tiles = each(lambda size: (N_LAT, padded(2 * size), LANES), BF16)
    slabs = each(lambda size: (LANES, N_LAT * 2 * size), BF16)
    table = pltpu.VMEM((16, M), F32)
    square = pltpu.VMEM((NLAT, NLAT), F32)
    owned = pltpu.VMEM((NLAT * EACH, LANES), F32)
    return pl.pallas_call(
        kernel,
        out_shape=jax.ShapeDtypeStruct(fields.shape, BF16),
        in_specs=[smem] * 5 + [vmem, vmem, pl.BlockSpec(memory_space=pl.ANY)],
        out_specs=vmem,
        scratch_shapes=[
            pltpu.VMEM((EACH, NLAT, M), F32),
            pltpu.VMEM((2, FL, K0), F32),
            each(lambda size: (2, KK * size, K0), F32),
            block, block,
            pltpu.VMEM((K0, 2 * M), BF16),
            pltpu.VMEM((32, M), F32), pltpu.VMEM((32, M), F32),
            table, table, table, table,
            pltpu.VMEM((2, 8, M), F32),
            acc, acc,
            pltpu.VMEM((padded(2 * max(SIZES)), M), F32),
            tiles, tiles,
            pltpu.VMEM((N_LAT * 2 * max(SIZES), LANES), F32),
            slabs, slabs,
            owned, owned,
            slabs, slabs,
            tiles, tiles,
            square, square, square,
            pltpu.VMEM((3 * NLAT, M), BF16),
            pltpu.VMEM((EACH, 3 * NLAT, NLAT), BF16),
            acc, acc,
            block, block,
            pltpu.VMEM((FL, M), F32),
            dma,
            dma((2, N_LEV)), dma((2, N_LEV)), dma((2, N_LEV)), dma((2, N_LEV)),
            dma((2, 4, 2)),
        ],
        compiler_params=pltpu.CompilerParams(
            collective_id=0, has_side_effects=True, vmem_limit_bytes=56 * 1024 * 1024
        ),
        cost_estimate=pl.CostEstimate(
            flops=20_000_000_000, bytes_accessed=12_000_000, transcendentals=0
        ),
    )(lat_order, counts, wave_order, weights, diffusion, wave_order.reshape(1, M), fields, legendre)


def solution(mesh):
    placed = (P("lat", None, "lev"), P(), P(), P(), P(), P(), P(("lat", "lev"), None, None))
    return jax.shard_map(
        body, mesh=mesh, in_specs=placed, out_specs=P("lat", None, "lev"), check_vma=False
    )
```

```python
import math

import jax
import jax.numpy as jnp
from jax import lax
from jax.experimental import pallas as pl
from jax.experimental.pallas import tpu as pltpu
from jax.sharding import PartitionSpec as P

F32, BF16 = jnp.float32, jnp.bfloat16
MESH = pl.DeviceIdType.MESH

M = 2048
N_LAT, N_LEV = 16, 8
DEV = N_LAT * N_LEV
NLAT = 64
LEV = 24
FL = 72
HALF = FL // 2
ROWS = NLAT // N_LAT
PTS = 2048
K0 = 256
KK = PTS // K0
PAIRS = KK // 2
EACH = M // DEV
WT = 256
LANES = 128
SIZES = (20, 16)
STARTS = (0, 20)
CHUNKS = range(len(SIZES))
SLOT = 64


def padded(rows):
    return -(-rows // 16) * 16


def nt_dot(a, b):
    return lax.dot_general(a, b, (((1,), (1,)), ((), ())), preferred_element_type=F32)


def sincos(wave, factor, count):
    product = wave * factor
    countf = count.astype(F32)
    turns = jnp.floor(product.astype(F32) * (1.0 / countf) + 0.5).astype(jnp.int32)
    rest = product - turns * count
    rest = jnp.where(2 * rest > count, rest - count, rest)
    rest = jnp.where(2 * rest < -count, rest + count, rest)
    z = rest.astype(F32) * (math.pi / countf)
    y = z * z
    s = jnp.full_like(y, 1.0 / math.factorial(13))
    for k in (11, 9, 7, 5, 3, 1):
        s = s * y + (-1.0) ** (k // 2) / math.factorial(k)
    s = s * z
    c = jnp.full_like(y, 1.0 / math.factorial(14) * -1.0)
    for k in (12, 10, 8, 6, 4, 2, 0):
        c = c * y + (-1.0) ** (k // 2) / math.factorial(k)
    return 1.0 - 2.0 * s * s, 2.0 * s * c


def kernel(
    lat_s, cnt_s, wave_s, wgt_s, dif_s, wave_v, fields, leg_hbm, out,
    leg, tmp, stages, xs, xr, basis, twc, tws, ebc, ebs, eac, eas, one,
    accr, acci, ft, fs, f1, mid, m1, f2, x32, y32, g1, g2, gs, g3,
    pm, cn, wt, bs, gst, ur, ui, ys, yr, o32,
    leg_sem, xs_sem, xr_sem, ys_sem, yr_sem, tile_sem,
):
    lat, lev = lax.axis_index("lat"), lax.axis_index("lev")
    z = lev // 2

    barrier = pltpu.get_barrier_semaphore()

    def greet_lev(d, carry):
        pl.semaphore_signal(
            barrier, inc=1, device_id=(lat, lax.rem(lev + d, N_LEV)), device_id_type=MESH
        )
        return carry

    def greet_lat(d, carry):
        pl.semaphore_signal(
            barrier, inc=1, device_id=(lax.rem(lat + d, N_LAT), lev), device_id_type=MESH
        )
        return carry

    lax.fori_loop(1, N_LEV, greet_lev, 0)
    lax.fori_loop(1, N_LAT, greet_lat, 0)
    leg_copy = pltpu.make_async_copy(leg_hbm, leg, leg_sem)
    leg_copy.start()

    lane = lax.broadcasted_iota(jnp.int32, (FL, K0), 1)

    def stage_row(t, carry):
        count = cnt_s[lat_s[ROWS * lat + t]]
        for kk in range(KK):
            x = fields[t, :, kk * K0 : (kk + 1) * K0].astype(F32)
            tmp[kk % 2] = jnp.where(lane + (lev * PTS + kk * K0) < count, x, 0.0)
            for n in CHUNKS:
                for h in range(2):
                    first = h * HALF + STARTS[n]
                    stages[n][h, kk * SIZES[n] : (kk + 1) * SIZES[n], :] = tmp[
                        kk % 2, first : first + SIZES[n], :
                    ]
        for n in CHUNKS:
            for h in range(2):
                xs[n][2 * t + h] = stages[n][h].astype(BF16)
        return carry

    lax.fori_loop(0, ROWS, stage_row, 0)

    pl.semaphore_wait(barrier, N_LEV - 1 + N_LAT - 1)

    def x_copy(n, target, source):
        return pltpu.make_async_remote_copy(
            src_ref=xs[n].at[target],
            dst_ref=xr[n].at[source],
            send_sem=xs_sem.at[n, target],
            recv_sem=xr_sem.at[n, source],
            device_id=(lat, target),
            device_id_type=MESH,
        )

    other = lev + 1 - 2 * lax.rem(lev, 2)

    def partner(step):
        chip_step = step // 2
        far = jnp.where(chip_step == 0, 1, jnp.where(chip_step == 1, 3, 2))
        return 2 * lax.rem(z + far, 4) + lax.rem(lev + lax.rem(step, 2), 2)

    def points_send(n):
        x_copy(n, other, lev).start()

        def send_x(step, carry):
            x_copy(n, partner(step), lev).start()
            return carry

        lax.fori_loop(0, 6, send_x, 0)

    points_send(0)

    count = cnt_s[lat_s[ROWS * lat + z]]
    waves16 = jnp.broadcast_to(wave_v[...], (16, M))
    row16 = lax.broadcasted_iota(jnp.int32, (16, M), 0)
    ebc[...], ebs[...] = sincos(waves16, row16, count)
    eac[...], eas[...] = sincos(waves16, row16 * 16, count)
    twc[0:16], tws[0:16] = sincos(waves16, row16 * (2 * K0), count)
    twc[16:32], tws[16:32] = sincos(waves16, row16 * (2 * K0) + 32 * K0, count)
    waves8 = jnp.broadcast_to(wave_v[...], (8, M))
    one[0], one[1] = sincos(waves8, jnp.full((8, M), K0, jnp.int32), count)

    def basis_rows(a, carry):
        ca, sa = eac[pl.ds(a, 1), :], eas[pl.ds(a, 1), :]
        cb, sb = ebc[...], ebs[...]
        rows = pl.ds(pl.multiple_of(a * 16, 16), 16)
        basis[rows, 0:M] = (ca * cb - sa * sb).astype(BF16)
        basis[rows, M : 2 * M] = (-(sa * cb + ca * sb)).astype(BF16)
        return carry

    lax.fori_loop(0, 16, basis_rows, 0)

    lane64 = lax.broadcasted_iota(jnp.int32, (1, NLAT), 1)

    def slot_row(t, carry):
        j = lat_s[t]
        row = pl.ds(t, 1)
        pm[row, :] = jnp.where(lane64 == j, 1.0, 0.0)
        cn[row, :] = jnp.full((1, NLAT), cnt_s[j], jnp.int32).astype(F32)
        wt[row, :] = jnp.full((1, NLAT), wgt_s[j], F32)
        return carry

    lax.fori_loop(0, NLAT, slot_row, 0)
    eye = lax.broadcasted_iota(jnp.int32, (NLAT, NLAT), 0) == lax.broadcasted_iota(
        jnp.int32, (NLAT, NLAT), 1
    )
    count_col = cn[...]
    count_row = jnp.sum(jnp.where(eye, count_col, 0.0), axis=0, keepdims=True)
    share_row = jnp.sum(jnp.where(eye, wt[...], 0.0), axis=0, keepdims=True) / count_row
    perm = pm[...].astype(BF16)
    degree = lax.broadcasted_iota(jnp.int32, (1, M), 1)
    leg_copy.wait()

    def operator(i, carry):
        m = wave_s[(lat * N_LEV + lev) * EACH + i]
        deg = (degree + m).astype(F32)
        scaled = deg * (deg + 1.0) * (1.0 / float(M * (M - 1)))
        scaled = scaled * scaled
        own = jnp.dot(perm, leg[i].astype(BF16), preferred_element_type=F32)
        for f in range(3):
            bs[f * NLAT : (f + 1) * NLAT, :] = (own * (1.0 / (1.0 + dif_s[f] * scaled))).astype(BF16)
        g = nt_dot(bs[...], own.astype(BF16))
        twice_m = (2 * jnp.full((1, NLAT), m, jnp.int32)).astype(F32)
        from_row = jnp.where(twice_m < count_row, share_row, 0.0)
        to_col = jnp.where(twice_m < count_col, jnp.where(twice_m == 0.0, 1.0, 2.0), 0.0)
        scale = to_col * from_row
        for f in range(3):
            gst[i, f * NLAT : (f + 1) * NLAT, :] = (g[f * NLAT : (f + 1) * NLAT, :] * scale).astype(BF16)
        return carry

    def operators(first, last):
        lax.fori_loop(first, last, operator, 0)

    x32[...] = jnp.zeros_like(x32)
    ft[...] = jnp.zeros_like(ft)
    c1, s1 = one[0, 0:1, :], one[1, 0:1, :]

    def xy_copy(n, k, source, target_ref, d):
        target = lax.rem(lat + d, N_LAT)
        return pltpu.make_async_remote_copy(
            src_ref=source.at[target],
            dst_ref=target_ref.at[lat],
            send_sem=tile_sem.at[n, k, 0],
            recv_sem=tile_sem.at[n, k, 1],
            device_id=(target, lev),
            device_id_type=MESH,
        )

    def xy_send(n, k, source, target_ref):
        def step(d, carry):
            xy_copy(n, k, source, target_ref, d).start()
            return carry

        lax.fori_loop(1, N_LAT, step, 0)
        target_ref[lat] = source[lat]

    def xy_all(n, k, source, target_ref):
        return pltpu.make_async_remote_copy(
            src_ref=source.at[pl.ds(0, N_LAT - 1)],
            dst_ref=target_ref.at[pl.ds(0, N_LAT - 1)],
            send_sem=tile_sem.at[n, k, 0],
            recv_sem=tile_sem.at[n, k, 1],
            device_id=(lax.rem(lat + 1, N_LAT), lev),
            device_id_type=MESH,
        )

    def slab(index):
        return pl.ds(pl.multiple_of(index * EACH, EACH), EACH)

    def z_send(n, k, source, target_ref):
        def step(d, carry):
            target = lax.rem(lev + d, N_LEV)
            pltpu.make_async_remote_copy(
                src_ref=source.at[slab(target), :],
                dst_ref=target_ref.at[slab(lev), :],
                send_sem=tile_sem.at[n, k, 0],
                recv_sem=tile_sem.at[n, k, 1],
                device_id=(lat, target),
                device_id_type=MESH,
            ).start()
            return carry

        lax.fori_loop(1, N_LEV, step, 0)
        target_ref[slab(lev), :] = source[slab(lev), :]

    def z_all(n, k, source, target_ref):
        whole = pl.ds(0, (N_LEV - 1) * EACH)
        return pltpu.make_async_remote_copy(
            src_ref=source.at[whole, :],
            dst_ref=target_ref.at[whole, :],
            send_sem=tile_sem.at[n, k, 0],
            recv_sem=tile_sem.at[n, k, 1],
            device_id=(lat, lax.rem(lev + 1, N_LEV)),
            device_id_type=MESH,
        )

    def chip_at(step):
        far = jnp.where(step == 0, 0, jnp.where(step == 1, 3, jnp.where(step == 2, 1, 2)))
        return lax.rem(z + far, 4)

    def forward_start(n):
        accr[n][...] = jnp.zeros_like(accr[n])
        acci[n][...] = jnp.zeros_like(acci[n])
        xr[n][lev] = xs[n][lev]

    def forward(n, first, last):
        columns = 2 * SIZES[n]

        def step(index, carry):
            chip = chip_at(index)
            for q in range(2):
                p = 2 * chip + q

                @pl.when(p != lev)
                def _(p=p):
                    x_copy(n, p, p).wait_recv()

            points = xr[n][pl.ds(2 * chip, 2)].reshape(2 * KK * SIZES[n], K0)
            for w in range(M // WT):
                cols = slice(w * WT, (w + 1) * WT)
                pr = jnp.dot(points, basis[:, cols], preferred_element_type=F32)
                pi = jnp.dot(points, basis[:, M + w * WT : M + (w + 1) * WT], preferred_element_type=F32)
                ar, ai = accr[n][:, cols], acci[n][:, cols]
                for k in range(2 * PAIRS):
                    c = twc[pl.ds(chip * (2 * PAIRS) + k, 1), cols]
                    s = tws[pl.ds(chip * (2 * PAIRS) + k, 1), cols]
                    br, bi = pr[k * columns : (k + 1) * columns], pi[k * columns : (k + 1) * columns]
                    ar = ar + (br * c + bi * s)
                    ai = ai + (bi * c - br * s)
                accr[n][:, cols] = ar
                acci[n][:, cols] = ai
            return carry

        lax.fori_loop(first, last, step, 0)

    def forward_end(n):
        size, columns = SIZES[n], 2 * SIZES[n]
        odd_r, odd_i = accr[n][size:columns, :], acci[n][size:columns, :]
        ft[0:size, :] = accr[n][0:size, :] + (odd_r * c1 + odd_i * s1)
        ft[size:columns, :] = acci[n][0:size, :] + (odd_i * c1 - odd_r * s1)
        for w in range(N_LAT):
            fs[n][w] = ft[0 : padded(columns), w * LANES : (w + 1) * LANES].astype(BF16)
        xy_send(n, 0, fs[n], f1[n])

    def middle(n):
        columns = 2 * SIZES[n]
        xy_all(n, 0, fs[n], f1[n]).wait_recv()
        for r in range(N_LAT):
            mid[r * columns : (r + 1) * columns, :] = f1[n][r].astype(F32)[0:columns, :]
        for j in range(N_LAT * columns // LANES):
            cols = slice(j * LANES, (j + 1) * LANES)
            m1[n][:, cols] = mid[cols, :].T.astype(BF16)
        z_send(n, 1, m1[n], f2[n])

    def apply(n):
        size, columns = SIZES[n], 2 * SIZES[n]
        z_all(n, 1, m1[n], f2[n]).wait_recv()
        for source in range(N_LEV):
            v = f2[n][source * EACH : (source + 1) * EACH, :].astype(F32)
            lanes = slice((source % 2) * SLOT, (source % 2) * SLOT + columns)
            for r in range(N_LAT):
                t = r * ROWS + source // 2
                x32[t * EACH : (t + 1) * EACH, lanes] = v[:, r * columns : (r + 1) * columns]
        column = lax.broadcasted_iota(jnp.int32, (NLAT, LANES), 1)
        level = STARTS[n] + jnp.where(column >= SLOT, column - SLOT + HALF, column)
        inside = jnp.where(column >= SLOT, column - SLOT, column)
        level = jnp.where(inside >= size, level - size, level)
        for i in range(EACH):
            x = x32[pl.ds(i, NLAT, stride=EACH), :].astype(BF16)
            y = jnp.dot(gst[i], x, preferred_element_type=F32)
            y32[pl.ds(i, NLAT, stride=EACH), :] = jnp.where(
                level < LEV, y[0:NLAT], jnp.where(level < 2 * LEV, y[NLAT : 2 * NLAT], y[2 * NLAT :])
            )
        for target in range(N_LEV):
            lanes = slice((target % 2) * SLOT, (target % 2) * SLOT + columns)
            pieces = []
            for r in range(N_LAT):
                t = r * ROWS + target // 2
                pieces.append(y32[t * EACH : (t + 1) * EACH, lanes])
            g1[n][target * EACH : (target + 1) * EACH, :] = jnp.concatenate(pieces, axis=1).astype(BF16)
        z_send(n, 2, g1[n], g2[n])

    def middle_back(n):
        columns = 2 * SIZES[n]
        z_all(n, 2, g1[n], g2[n]).wait_recv()
        for j in range(N_LAT * columns // LANES):
            cols = slice(j * LANES, (j + 1) * LANES)
            mid[cols, :] = g2[n][:, cols].astype(F32).T
        for r in range(N_LAT):
            block = mid[r * columns : (r + 1) * columns, :]
            if padded(columns) > columns:
                block = jnp.concatenate([block, jnp.zeros((padded(columns) - columns, LANES), F32)], axis=0)
            gs[n][r] = block.astype(BF16)
        xy_send(n, 3, gs[n], g3[n])

    def inverse_start(n):
        size, columns = SIZES[n], 2 * SIZES[n]
        xy_all(n, 3, gs[n], g3[n]).wait_recv()
        for w in range(N_LAT):
            ft[0:columns, w * LANES : (w + 1) * LANES] = g3[n][w].astype(F32)[0:columns, :]
        re, im = ft[0:size, :], ft[size:columns, :]
        ur[n][0:size, :] = re
        ui[n][0:size, :] = im
        ur[n][size:columns, :] = re * c1 - im * s1
        ui[n][size:columns, :] = re * s1 + im * c1

    def y_copy(n, target, source):
        return pltpu.make_async_remote_copy(
            src_ref=ys[n].at[target],
            dst_ref=yr[n].at[source],
            send_sem=ys_sem.at[n, target],
            recv_sem=yr_sem.at[n, source],
            device_id=(lat, target),
            device_id_type=MESH,
        )

    def inverse(n, first, last):
        rows = 2 * KK * SIZES[n]
        row = lax.broadcasted_iota(jnp.int32, (rows, K0), 0)
        point = lax.broadcasted_iota(jnp.int32, (rows, K0), 1)
        for kk in range(1, 2 * KK):
            point = point + jnp.where(row >= kk * SIZES[n], K0, 0)

        def step(index, carry):
            chip = chip_at(3 - index)
            total = jnp.zeros((rows, K0), F32)
            for w in range(M // WT):
                cols = slice(w * WT, (w + 1) * WT)
                vr, vi = ur[n][:, cols], ui[n][:, cols]
                tr, ti = [], []
                for k in range(2 * PAIRS):
                    c = twc[pl.ds(chip * (2 * PAIRS) + k, 1), cols]
                    s = tws[pl.ds(chip * (2 * PAIRS) + k, 1), cols]
                    tr.append(vr * c - vi * s)
                    ti.append(vr * s + vi * c)
                total = total + nt_dot(jnp.concatenate(tr, axis=0).astype(BF16), basis[:, cols])
                total = total + nt_dot(
                    jnp.concatenate(ti, axis=0).astype(BF16), basis[:, M + w * WT : M + (w + 1) * WT]
                )
            total = jnp.where(point + chip * (2 * PTS) < count, total, 0.0).astype(BF16)
            for q in range(2):
                p = 2 * chip + q
                ys[n][p] = total[q * (rows // 2) : (q + 1) * (rows // 2)]

                @pl.when(p != lev)
                def _(p=p):
                    y_copy(n, p, lev).start()

            return carry

        lax.fori_loop(first, last, step, 0)

    operators(0, 10)
    points_send(1)
    forward_start(0)
    forward(0, 0, 4)
    forward_end(0)
    operators(10, 16)
    middle(0)
    forward_start(1)
    forward(1, 0, 4)
    forward_end(1)
    apply(0)
    middle(1)
    middle_back(0)
    apply(1)
    inverse_start(0)
    inverse(0, 0, 2)
    middle_back(1)
    inverse(0, 2, 4)
    inverse_start(1)
    inverse(1, 0, 4)

    for n in CHUNKS:
        yr[n][lev] = ys[n][lev]

        def waited(d, carry, n=n):
            y_copy(n, lev, lax.rem(lev + d, N_LEV)).wait_recv()
            return carry

        lax.fori_loop(1, N_LEV, waited, 0)

    def finish_row(t, carry):
        for n in CHUNKS:
            for h in range(2):
                stages[n][h] = yr[n][2 * t + h].astype(F32)
                first = h * HALF + STARTS[n]
                for kk in range(KK):
                    o32[first : first + SIZES[n], kk * K0 : (kk + 1) * K0] = stages[n][
                        h, kk * SIZES[n] : (kk + 1) * SIZES[n], :
                    ]
        out[t] = o32[...].astype(BF16)
        return carry

    lax.fori_loop(0, ROWS, finish_row, 0)

    for n in CHUNKS:

        def sent(d, carry, n=n):
            target = lax.rem(lev + d, N_LEV)
            x_copy(n, target, lev).wait_send()
            y_copy(n, target, lev).wait_send()
            return carry

        lax.fori_loop(1, N_LEV, sent, 0)
        xy_all(n, 0, fs[n], f1[n]).wait_send()
        z_all(n, 1, m1[n], f2[n]).wait_send()
        z_all(n, 2, g1[n], g2[n]).wait_send()
        xy_all(n, 3, gs[n], g3[n]).wait_send()


def body(fields, lat_order, counts, wave_order, weights, diffusion, legendre):
    smem, vmem = pl.BlockSpec(memory_space=pltpu.SMEM), pl.BlockSpec(memory_space=pltpu.VMEM)
    dma = pltpu.SemaphoreType.DMA

    def each(shape, dtype):
        return tuple(pltpu.VMEM(shape(size), dtype) for size in SIZES)

    block = each(lambda size: (N_LEV, KK * size, K0), BF16)
    acc = each(lambda size: (2 * size, M), F32)
    tiles = each(lambda size: (N_LAT, padded(2 * size), LANES), BF16)
    slabs = each(lambda size: (LANES, N_LAT * 2 * size), BF16)
    table = pltpu.VMEM((16, M), F32)
    square = pltpu.VMEM((NLAT, NLAT), F32)
    owned = pltpu.VMEM((NLAT * EACH, LANES), F32)
    return pl.pallas_call(
        kernel,
        out_shape=jax.ShapeDtypeStruct(fields.shape, BF16),
        in_specs=[smem] * 5 + [vmem, vmem, pl.BlockSpec(memory_space=pl.ANY)],
        out_specs=vmem,
        scratch_shapes=[
            pltpu.VMEM((EACH, NLAT, M), F32),
            pltpu.VMEM((2, FL, K0), F32),
            each(lambda size: (2, KK * size, K0), F32),
            block, block,
            pltpu.VMEM((K0, 2 * M), BF16),
            pltpu.VMEM((32, M), F32), pltpu.VMEM((32, M), F32),
            table, table, table, table,
            pltpu.VMEM((2, 8, M), F32),
            acc, acc,
            pltpu.VMEM((padded(2 * max(SIZES)), M), F32),
            tiles, tiles,
            pltpu.VMEM((N_LAT * 2 * max(SIZES), LANES), F32),
            slabs, slabs,
            owned, owned,
            slabs, slabs,
            tiles, tiles,
            square, square, square,
            pltpu.VMEM((3 * NLAT, M), BF16),
            pltpu.VMEM((EACH, 3 * NLAT, NLAT), BF16),
            acc, acc,
            block, block,
            pltpu.VMEM((FL, M), F32),
            dma,
            dma((2, N_LEV)), dma((2, N_LEV)), dma((2, N_LEV)), dma((2, N_LEV)),
            dma((2, 4, 2)),
        ],
        compiler_params=pltpu.CompilerParams(
            collective_id=0, has_side_effects=True, vmem_limit_bytes=56 * 1024 * 1024
        ),
        cost_estimate=pl.CostEstimate(
            flops=20_000_000_000, bytes_accessed=12_000_000, transcendentals=0
        ),
    )(lat_order, counts, wave_order, weights, diffusion, wave_order.reshape(1, M), fields, legendre)


def solution(mesh):
    placed = (P("lat", None, "lev"), P(), P(), P(), P(), P(), P(("lat", "lev"), None, None))
    return jax.shard_map(
        body, mesh=mesh, in_specs=placed, out_specs=P("lat", None, "lev"), check_vma=False
    )
```
